512 devices in a mesh: ctx: 16 (over z, core), kvh: 8 (over y), tp: 4 (over x).
Axes of the slice: x: 4, y: 8, z: 8, core: 2. Of those that a mesh axis runs over, the one named last changes fastest.
Arguments:
- prefill_cache: bfloat16 [2, 32, 8192, 1024], P(None, None, ('ctx', 'tp'), 'kvh'), may hold values from -4 to 4
- lengths: int32 [32], replicated, may hold values from 1 to 8192, 163840 in all
- slot_of: int32 [32], replicated, may hold values from 0 to 31, each once
- queries: bfloat16 [4, 32, 16384], P(None, 'ctx', ('kvh', 'tp')), may hold values from -100 to 100
- new_kv: bfloat16 [2, 4, 32, 1024], P(None, None, 'ctx', 'kvh'), may hold values from -4 to 4
Outputs:
- attended: bfloat16 [4, 32, 16384], P(None, 'ctx', ('kvh', 'tp'))
- decode_cache: bfloat16 [2, 32, 8192, 1024], P(None, 'ctx', 'tp', 'kvh')
The draws below stay inside these ranges and needn't reach their ends.
Inputs may be any that keep to these rules, and one draw needn't show every extreme that they name: `lengths`: each request has at least one live position; the longest request fills all 8192 slots. `slot_of`: each slot is given to exactly one request.
All inputs are finite; a program needn't handle non-finite values.
Results may differ from the reference program's by a relative error of at most 0.011.
Values may be sent and summed in bfloat16 or wider, within the bound.
A program may use at most 64 MiB of HBM per device.

```python
import math
import jax
import jax.numpy as jnp
import numpy as np
from jax import lax

QH = 128
KVH = 8
HD = 128
LMAX = 8192
STEPS = 4
R = 32
BLOCK = 128
N_CTX = 16
N_TP = 4


def shared_fresh(key):
    return jnp.clip(jax.random.normal(key, (2, STEPS, R, KVH * HD), jnp.float32), -4.0, 4.0)


def draw_new_kv(key, part):
    fresh = shared_fresh(key)
    return fresh.astype(jnp.bfloat16)


def draw_queries(key, part):
    key = jax.random.fold_in(key, 3)
    base = jnp.clip(jax.random.normal(key, (STEPS, R, QH * HD), jnp.float32), -4.0, 4.0)
    return base.astype(jnp.bfloat16)


def block_scale(key, extent, cuts, least, top_value):
    level = 1.0
    for position, blocks in cuts:
        heights = jax.random.uniform(jax.random.fold_in(jax.random.fold_in(key, 6), position), (blocks,), jnp.float32, least / len(cuts), top_value / len(cuts))
        level = level * jnp.repeat(jnp.exp(heights), extent[position] // blocks).reshape((-1,) + (1,) * (len(extent) - 1 - position))
    return level


def split_up(amount, total, bound, slope):
    loads = [(1 << 20) // math.isqrt(rank ** slope) + 1 for rank in range(2, amount + 1)]
    surplus, counts = total - bound - (amount - 1), [1] * (amount - 1)
    while surplus > 0:
        free = [i for i in range(amount - 1) if counts[i] < bound]
        pool, budget = sum([loads[i] for i in free]), surplus
        for i in free:
            extra = min(bound - counts[i], max(1, budget * loads[i] // pool), surplus)
            counts[i] = counts[i] + extra
            surplus = surplus - extra
    return np.array([bound] + counts)


def uneven_parts(stream_key, amount, total, reach, lean):
    if amount == 2:
        one = jax.random.randint(stream_key, (), max(1, total - reach), min(reach, total - 1) + 1)
        return jnp.stack([one, total - one])
    sizes = jnp.asarray(split_up(amount, total, reach, lean), jnp.int32)
    couples = (amount - 1) // 2
    source_of, sink = sizes[1:1 + 2 * couples:2], sizes[2:2 + 2 * couples:2]
    slack = jnp.minimum(source_of - 1, reach - sink)
    moved = jax.random.randint(jax.random.fold_in(stream_key, 1), (couples,), 0, 1 << 20) % (slack + 1)
    sizes = sizes.at[1:1 + 2 * couples:2].set(source_of - moved).at[2:2 + 2 * couples:2].set(sink + moved)
    return sizes[jax.random.permutation(jax.random.fold_in(stream_key, 2), amount)]


def scatter_about(key, shape, spread, most, shards=(), kind=jnp.bfloat16):
    factor_of = block_scale(key, shape, shards, -0.22, 0.18) if shards else 1.0
    values = jax.random.normal(key, shape, jnp.float32) * spread * factor_of
    return jnp.minimum(jnp.maximum(values, -most), most).astype(kind)


def setup_inputs(seed: int = 0) -> dict:
    key_list = jax.random.split(jax.random.key(seed), 6)
    return {
        "prefill_cache": scatter_about(key_list[0], (2, R, LMAX, KVH * HD), 1.0, 4.0, ((2, 64), (3, 8))),
        "lengths": uneven_parts(key_list[1], R, R * LMAX * 5 // 8, LMAX, 2).astype(jnp.int32),
        "slot_of": jax.random.permutation(key_list[2], R).astype(jnp.int32),
        "queries": draw_queries(jax.random.fold_in(key_list[5], 71), 0),
        "new_kv": draw_new_kv(jax.random.fold_in(key_list[5], 71), 0),
    }


def reference(prefill_cache, lengths, slot_of, queries, new_kv):
    scale = 1.0 / math.sqrt(HD)
    group = QH // KVH
    order = jnp.arange(R, dtype=jnp.int32)
    inverse = lax.optimization_barrier(jnp.sum(jnp.where(slot_of[None, :] == order[:, None], order[None, :], 0), axis=1)).astype(jnp.int32)
    steps_idx = jnp.arange(STEPS, dtype=jnp.int32)
    causal = steps_idx[None, :] <= steps_idx[:, None]
    positions = jnp.arange(LMAX, dtype=jnp.int32)

    def one_request(index):
        place = slot_of[index]
        cache_rows = lax.dynamic_index_in_dim(prefill_cache, index, 1, keepdims=False)
        key_rows = cache_rows[0].reshape(LMAX, KVH, HD).astype(jnp.float32)
        value_rows = cache_rows[1].reshape(LMAX, KVH, HD).astype(jnp.float32)
        query_rows = lax.dynamic_index_in_dim(queries, place, 1, keepdims=False)
        query_rows = query_rows.reshape(STEPS, KVH, group, HD).astype(jnp.float32)
        fresh = lax.dynamic_index_in_dim(new_kv, place, 2, keepdims=False)
        fresh_keys = fresh[0].reshape(STEPS, KVH, HD).astype(jnp.float32)
        fresh_values = fresh[1].reshape(STEPS, KVH, HD).astype(jnp.float32)
        live = positions < lengths[index]
        old_scores = jnp.einsum('skgd,pkd->kgsp', query_rows, key_rows) * scale
        old_scores = jnp.where(live, old_scores, -1e+30)
        new_scores = jnp.einsum('skgd,ukd->kgsu', query_rows, fresh_keys) * scale
        new_scores = jnp.where(causal, new_scores, -1e+30)
        top = jnp.maximum(lax.optimization_barrier(jnp.max(old_scores, axis=-1)), lax.optimization_barrier(jnp.max(new_scores, axis=-1)))
        old_weights = jnp.where(live, jnp.exp(old_scores - top[..., None]), 0.0)
        new_weights = jnp.where(causal, jnp.exp(new_scores - top[..., None]), 0.0)
        total = lax.optimization_barrier(jnp.sum(old_weights, axis=-1)) + lax.optimization_barrier(jnp.sum(new_weights, axis=-1))
        rounded_old = lax.optimization_barrier(old_weights.astype(jnp.bfloat16)).astype(jnp.float32)
        rounded_new = lax.optimization_barrier(new_weights.astype(jnp.bfloat16)).astype(jnp.float32)
        summed = jnp.einsum('kgsp,pkd->kgsd', rounded_old, value_rows)
        summed = summed + jnp.einsum('kgsu,ukd->kgsd', rounded_new, fresh_values)
        result = summed / total[..., None]
        return jnp.transpose(result, (2, 0, 1, 3)).reshape(STEPS, QH * HD).astype(jnp.bfloat16)
    by_request = lax.map(one_request, order)
    by_slot = jnp.take(by_request, inverse, axis=0)
    attended = jnp.transpose(by_slot, (1, 0, 2))
    slot_cache = jnp.take(prefill_cache, inverse, axis=1)
    slot_cache = slot_cache.reshape(2, R, N_CTX, N_TP, BLOCK, KVH * HD)
    decode_cache = jnp.transpose(slot_cache, (0, 1, 3, 2, 4, 5)).reshape(2, R, LMAX, KVH * HD)
    return (attended, decode_cache)
```

```python
import math

import jax
import jax.numpy as jnp
from jax import lax
from jax.experimental import pallas as pl
from jax.experimental.pallas import tpu as pltpu
from jax.sharding import PartitionSpec as P

HD = 128
STEPS = 4
SCALE = 1.0 / math.sqrt(HD)
MESH = pl.DeviceIdType.MESH
DEAD = -1e38
FLOOR = -1e30


def kernel(
    cache_ref, slot_ref, len_ref, query_ref, new_ref,
    out_ref, rec_ref,
    raw, stage, own_q, all_q, mail, running, box,
    load_sem, send_sem, recv_sem, q_send_sem, q_recv_sem, mail_send_sem, mail_recv_sem,
):
    me = lax.axis_index("ctx")
    tp = lax.axis_index("tp")
    z, core = me // 2, lax.rem(me, 2)
    n_ctx = lax.axis_size("ctx")
    n_tp = lax.axis_size("tp")
    chips = n_ctx // 2
    requests = slot_ref.shape[0]
    slots = requests // n_ctx
    block = cache_ref.shape[2]
    own_heads = query_ref.shape[2] // HD
    rows = STEPS * own_heads

    load = pltpu.make_async_copy(cache_ref, raw, load_sem)
    load.start()

    def partner(dz, other):
        return lax.rem(z + dz, chips) * 2 + (1 - core if other else core)

    barrier = pltpu.get_barrier_semaphore()
    for k in range(1, n_ctx):
        pl.semaphore_signal(
            barrier, inc=1, device_id={"ctx": lax.rem(me + k, n_ctx)}, device_id_type=MESH
        )
    for k in range(1, n_tp):
        pl.semaphore_signal(
            barrier, inc=1, device_id={"tp": lax.rem(tp + k, n_tp)}, device_id_type=MESH
        )

    for j in range(slots):
        for s in range(STEPS):
            for h in range(own_heads):
                own_q[j, s * own_heads + h, :] = query_ref[
                    s, j, h * HD : (h + 1) * HD
                ].astype(jnp.float32)
    all_q[:, pl.ds(tp * rows, rows), :] = own_q[...].astype(jnp.bfloat16)

    def request_of(slot):
        found = jnp.int32(0)
        for r in range(1, requests):
            found = jnp.where(slot_ref[r] == slot, r, found)
        return found

    def fill(d):
        for j in range(slots):
            r = request_of(d * slots + j)
            for k in range(2):
                stage[d, k, j] = raw[k, r]

    def to(d):
        return pltpu.make_async_remote_copy(
            src_ref=stage.at[d],
            dst_ref=rec_ref.at[:, :, pl.ds(me * block, block)],
            send_sem=send_sem.at[d],
            recv_sem=recv_sem.at[me],
            device_id={"ctx": d},
            device_id_type=MESH,
        )

    def arrived(d):
        pltpu.make_async_remote_copy(
            src_ref=stage.at[d],
            dst_ref=rec_ref.at[:, :, pl.ds(d * block, block)],
            send_sem=send_sem.at[d],
            recv_sem=recv_sem.at[d],
            device_id={"ctx": d},
            device_id_type=MESH,
        ).wait_recv()

    def q_copy(owner, t):
        here = all_q.at[:, pl.ds(owner * rows, rows)]
        return pltpu.make_async_remote_copy(
            src_ref=here, dst_ref=here,
            send_sem=q_send_sem.at[t], recv_sem=q_recv_sem.at[owner],
            device_id={"tp": t}, device_id_type=MESH,
        )

    def mail_copy(owner, t):
        return pltpu.make_async_remote_copy(
            src_ref=mail.at[:, :, pl.ds(t * rows, rows)], dst_ref=box.at[owner],
            send_sem=mail_send_sem.at[t], recv_sem=mail_recv_sem.at[owner],
            device_id={"tp": t}, device_id_type=MESH,
        )

    load.wait()
    first = partner(0, True)
    fill(first)
    pl.semaphore_wait(barrier, n_ctx - 1 + n_tp - 1)

    to(first).start()
    for k in range(1, n_tp):
        q_copy(tp, lax.rem(tp + k, n_tp)).start()

    def send_round(k, carry):
        for other in (False, True):
            for dz in (k, chips - k):
                d = partner(dz, other)
                fill(d)
                to(d).start()
        return carry

    lax.fori_loop(1, chips // 2, send_round, 0)
    for other in (False, True):
        d = partner(chips // 2, other)
        fill(d)
        to(d).start()

    fill(me)
    rec_ref[:, :, pl.ds(me * block, block), :] = stage[me]

    row_step = lax.broadcasted_iota(jnp.int32, (rows, HD), 0) // own_heads
    for j in range(slots):
        queries = own_q[j]
        scores = []
        for u in range(STEPS):
            key = new_ref[0, u, j, :].astype(jnp.float32).reshape(1, HD)
            dots = jnp.sum(queries * key, axis=1, keepdims=True)
            scores.append(jnp.where(row_step >= u, jnp.broadcast_to(dots, (rows, HD)), DEAD))
        top = scores[0]
        for u in range(1, STEPS):
            top = jnp.maximum(top, scores[u])
        total = jnp.zeros((rows, HD), jnp.float32)
        summed = jnp.zeros((rows, HD), jnp.float32)
        for u in range(STEPS):
            weight = jnp.exp((scores[u] - top) * SCALE)
            value = new_ref[1, u, j, :].astype(jnp.float32).reshape(1, HD)
            total = total + weight
            summed = summed + weight.astype(jnp.bfloat16).astype(jnp.float32) * value
        box[n_tp, 0, j] = summed
        box[n_tp, 1, j] = top
        running[2, j, 0:rows] = total

    lengths = [len_ref[request_of(me * slots + j)] for j in range(slots)]
    mail[0] = jnp.zeros(mail.shape[1:], jnp.float32)
    running[0] = jnp.full(running.shape[1:], FLOOR, jnp.float32)
    running[1] = jnp.zeros(running.shape[1:], jnp.float32)

    for k in range(1, n_tp):
        t = lax.rem(tp + k, n_tp)
        q_copy(t, t).wait_recv()

    span = 2 * block
    lane = lax.broadcasted_iota(jnp.int32, (n_tp * rows, span), 1)
    place = (lane // block) * (n_tp * block) + lax.rem(lane, block)

    def attend(chip):
        at = pl.ds(pl.multiple_of(chip * span, span), span)
        base = (chip * 2 * n_tp + tp) * block
        for j in range(slots):
            scores = lax.dot_general(
                all_q[j], rec_ref[0, j, at, :], (((1,), (1,)), ((), ())),
                preferred_element_type=jnp.float32,
            )
            scores = jnp.where(place < lengths[j] - base, scores, DEAD)
            before = running[0, j]
            top = jnp.maximum(before, jnp.max(scores, axis=1, keepdims=True))
            weights = jnp.exp((scores - jnp.concatenate([top, top], axis=1)) * SCALE)
            shrink = jnp.exp((before - top) * SCALE)
            running[0, j] = top
            running[1, j] = running[1, j] * shrink + jnp.sum(weights, axis=1, keepdims=True)
            mail[0, j] = mail[0, j] * shrink + jnp.dot(
                weights.astype(jnp.bfloat16), rec_ref[1, j, at, :],
                preferred_element_type=jnp.float32,
            )

    arrived(first)
    attend(z)

    def recv_round(k, carry):
        for dz in (k, chips - k):
            arrived(partner(dz, False))
            arrived(partner(dz, True))
            attend(lax.rem(z + dz, chips))
        return carry

    lax.fori_loop(1, chips // 2, recv_round, 0)
    arrived(partner(chips // 2, False))
    arrived(partner(chips // 2, True))
    attend(lax.rem(z + chips // 2, chips))

    half = lax.broadcasted_iota(jnp.int32, mail.shape[1:], 2) < HD // 2
    mail[1] = jnp.where(half, running[0], running[1])
    for k in range(1, n_tp):
        mail_copy(tp, lax.rem(tp + k, n_tp)).start()
    box[tp] = mail[:, :, pl.ds(tp * rows, rows), :]
    for k in range(1, n_tp):
        t = lax.rem(tp + k, n_tp)
        mail_copy(t, t).wait_recv()

    for j in range(slots):
        tops, totals = [], []
        for t in range(n_tp):
            both = box[t, 1, j]
            tops.append(jnp.broadcast_to(both[:, 0:1], (rows, HD)))
            totals.append(jnp.broadcast_to(both[:, HD // 2 : HD // 2 + 1], (rows, HD)))
        tops.append(box[n_tp, 1, j])
        totals.append(running[2, j, 0:rows])
        top = tops[0]
        for other in tops[1:]:
            top = jnp.maximum(top, other)
        total = jnp.zeros((rows, HD), jnp.float32)
        summed = jnp.zeros((rows, HD), jnp.float32)
        for t in range(n_tp + 1):
            share = jnp.exp((tops[t] - top) * SCALE)
            total = total + totals[t] * share
            summed = summed + box[t, 0, j] * share
        out_ref[j] = (summed / total).astype(out_ref.dtype)

    def sent(k, carry):
        to(lax.rem(me + k, n_ctx)).wait_send()
        return carry

    lax.fori_loop(1, n_ctx, sent, 0)
    for k in range(1, n_tp):
        t = lax.rem(tp + k, n_tp)
        q_copy(tp, t).wait_send()
        mail_copy(tp, t).wait_send()


def shards(prefill_cache, lengths, slot_of, queries, new_kv):
    n_ctx, n_tp = lax.axis_size("ctx"), lax.axis_size("tp")
    _, requests, block, width = prefill_cache.shape
    slots = requests // n_ctx
    own_heads = queries.shape[2] // HD
    rows = STEPS * own_heads
    attended, received = pl.pallas_call(
        kernel,
        out_shape=(
            jax.ShapeDtypeStruct((slots, rows, HD), jnp.bfloat16),
            jax.ShapeDtypeStruct((2, slots, n_ctx * block, width), jnp.bfloat16),
        ),
        in_specs=[
            pl.BlockSpec(memory_space=pltpu.HBM),
            pl.BlockSpec(memory_space=pltpu.SMEM),
            pl.BlockSpec(memory_space=pltpu.SMEM),
            pl.BlockSpec(memory_space=pltpu.VMEM),
            pl.BlockSpec(memory_space=pltpu.VMEM),
        ],
        out_specs=(
            pl.BlockSpec(memory_space=pltpu.VMEM),
            pl.BlockSpec(memory_space=pltpu.VMEM),
        ),
        scratch_shapes=[
            pltpu.VMEM(prefill_cache.shape, jnp.bfloat16),
            pltpu.VMEM((n_ctx, 2, slots, block, width), jnp.bfloat16),
            pltpu.VMEM((slots, rows, HD), jnp.float32),
            pltpu.VMEM((slots, n_tp * rows, HD), jnp.bfloat16),
            pltpu.VMEM((2, slots, n_tp * rows, HD), jnp.float32),
            pltpu.VMEM((3, slots, n_tp * rows, HD), jnp.float32),
            pltpu.VMEM((n_tp + 1, 2, slots, rows, HD), jnp.float32),
            pltpu.SemaphoreType.DMA,
            pltpu.SemaphoreType.DMA((n_ctx,)),
            pltpu.SemaphoreType.DMA((n_ctx,)),
            pltpu.SemaphoreType.DMA((n_tp,)),
            pltpu.SemaphoreType.DMA((n_tp,)),
            pltpu.SemaphoreType.DMA((n_tp,)),
            pltpu.SemaphoreType.DMA((n_tp,)),
        ],
        compiler_params=pltpu.CompilerParams(
            collective_id=0, has_side_effects=True, vmem_limit_bytes=32 << 20
        ),
        name="handover",
    )(prefill_cache, slot_of, lengths, queries, new_kv)
    attended = attended.reshape(slots, STEPS, own_heads * HD).transpose(1, 0, 2)
    return attended, received


def solution(mesh):
    return jax.shard_map(
        shards,
        mesh=mesh,
        in_specs=(
            P(None, None, ("ctx", "tp"), "kvh"),
            P(),
            P(),
            P(None, "ctx", ("kvh", "tp")),
            P(None, None, "ctx", "kvh"),
        ),
        out_specs=(P(None, "ctx", ("kvh", "tp")), P(None, "ctx", "tp", "kvh")),
        check_vma=False,
    )
```

```python
import math

import jax
import jax.numpy as jnp
from jax import lax
from jax.experimental import pallas as pl
from jax.experimental.pallas import tpu as pltpu
from jax.sharding import PartitionSpec as P

HD = 128
STEPS = 4
SCALE = 1.0 / math.sqrt(HD)
MESH = pl.DeviceIdType.MESH
DEAD = -1e38
FLOOR = -1e30


def kernel(
    cache_in, slot_in, len_in, query_in, new_in,
    out_ref, rec_ref,
    slot_ref, len_ref, query_ref, new_ref, raw, stage, own_q, all_q, mail, running, box,
    load_sem, send_sem, recv_sem, q_send_sem, q_recv_sem, mail_send_sem, mail_recv_sem,
):
    me = lax.axis_index("ctx")
    tp = lax.axis_index("tp")
    z, core = me // 2, lax.rem(me, 2)
    n_ctx = lax.axis_size("ctx")
    n_tp = lax.axis_size("tp")
    chips = n_ctx // 2
    requests = slot_ref.shape[0]
    slots = requests // n_ctx
    block = raw.shape[2]
    own_heads = query_ref.shape[2] // HD
    rows = STEPS * own_heads

    loads = [
        pltpu.make_async_copy(source, target, load_sem.at[i])
        for i, (source, target) in enumerate(
            [(slot_in, slot_ref), (cache_in, raw), (query_in, query_ref),
             (len_in, len_ref), (new_in, new_ref)]
        )
    ]
    for load in loads:
        load.start()

    def partner(dz, other):
        return lax.rem(z + dz, chips) * 2 + (1 - core if other else core)

    barrier = pltpu.get_barrier_semaphore()
    for k in range(1, n_ctx):
        pl.semaphore_signal(
            barrier, inc=1, device_id={"ctx": lax.rem(me + k, n_ctx)}, device_id_type=MESH
        )
    for k in range(1, n_tp):
        pl.semaphore_signal(
            barrier, inc=1, device_id={"tp": lax.rem(tp + k, n_tp)}, device_id_type=MESH
        )

    def request_of(slot):
        found = jnp.int32(0)
        for r in range(1, requests):
            found = jnp.where(slot_ref[r] == slot, r, found)
        return found

    def fill(d):
        for j in range(slots):
            r = request_of(d * slots + j)
            for k in range(2):
                stage[d, k, j] = raw[k, r]

    def to(d):
        return pltpu.make_async_remote_copy(
            src_ref=stage.at[d],
            dst_ref=rec_ref.at[:, :, pl.ds(me * block, block)],
            send_sem=send_sem.at[d],
            recv_sem=recv_sem.at[me],
            device_id={"ctx": d},
            device_id_type=MESH,
        )

    def arrived(d):
        pltpu.make_async_remote_copy(
            src_ref=stage.at[d],
            dst_ref=rec_ref.at[:, :, pl.ds(d * block, block)],
            send_sem=send_sem.at[d],
            recv_sem=recv_sem.at[d],
            device_id={"ctx": d},
            device_id_type=MESH,
        ).wait_recv()

    def q_copy(owner, t):
        here = all_q.at[:, pl.ds(owner * rows, rows)]
        return pltpu.make_async_remote_copy(
            src_ref=here, dst_ref=here,
            send_sem=q_send_sem.at[t], recv_sem=q_recv_sem.at[owner],
            device_id={"tp": t}, device_id_type=MESH,
        )

    def mail_copy(owner, t):
        return pltpu.make_async_remote_copy(
            src_ref=mail.at[:, :, pl.ds(t * rows, rows)], dst_ref=box.at[owner],
            send_sem=mail_send_sem.at[t], recv_sem=mail_recv_sem.at[owner],
            device_id={"tp": t}, device_id_type=MESH,
        )

    for load in loads:
        load.wait()
    first = partner(0, True)
    fill(first)

    for j in range(slots):
        for s in range(STEPS):
            for h in range(own_heads):
                own_q[j, s * own_heads + h, :] = query_ref[
                    s, j, h * HD : (h + 1) * HD
                ].astype(jnp.float32)
    all_q[:, pl.ds(tp * rows, rows), :] = own_q[...].astype(jnp.bfloat16)

    pl.semaphore_wait(barrier, n_ctx - 1 + n_tp - 1)

    to(first).start()
    for k in range(1, n_tp):
        q_copy(tp, lax.rem(tp + k, n_tp)).start()

    def send_round(k, carry):
        for other in (False, True):
            for dz in (k, chips - k):
                d = partner(dz, other)
                fill(d)
                to(d).start()
        return carry

    lax.fori_loop(1, chips // 2, send_round, 0)
    for other in (False, True):
        d = partner(chips // 2, other)
        fill(d)
        to(d).start()

    fill(me)
    rec_ref[:, :, pl.ds(me * block, block), :] = stage[me]

    row_step = lax.broadcasted_iota(jnp.int32, (rows, HD), 0) // own_heads
    for j in range(slots):
        queries = own_q[j]
        scores = []
        for u in range(STEPS):
            key = new_ref[0, u, j, :].astype(jnp.float32).reshape(1, HD)
            dots = jnp.sum(queries * key, axis=1, keepdims=True)
            scores.append(jnp.where(row_step >= u, jnp.broadcast_to(dots, (rows, HD)), DEAD))
        top = scores[0]
        for u in range(1, STEPS):
            top = jnp.maximum(top, scores[u])
        total = jnp.zeros((rows, HD), jnp.float32)
        summed = jnp.zeros((rows, HD), jnp.float32)
        for u in range(STEPS):
            weight = jnp.exp((scores[u] - top) * SCALE)
            value = new_ref[1, u, j, :].astype(jnp.float32).reshape(1, HD)
            total = total + weight
            summed = summed + weight.astype(jnp.bfloat16).astype(jnp.float32) * value
        box[n_tp, 0, j] = summed
        box[n_tp, 1, j] = top
        running[2, j, 0:rows] = total

    lengths = [len_ref[request_of(me * slots + j)] for j in range(slots)]
    mail[0] = jnp.zeros(mail.shape[1:], jnp.float32)
    running[0] = jnp.full(running.shape[1:], FLOOR, jnp.float32)
    running[1] = jnp.zeros(running.shape[1:], jnp.float32)

    for k in range(1, n_tp):
        t = lax.rem(tp + k, n_tp)
        q_copy(t, t).wait_recv()

    span = 2 * block
    lane = lax.broadcasted_iota(jnp.int32, (n_tp * rows, span), 1)
    place = (lane // block) * (n_tp * block) + lax.rem(lane, block)

    def attend(chip):
        at = pl.ds(pl.multiple_of(chip * span, span), span)
        base = (chip * 2 * n_tp + tp) * block
        for j in range(slots):
            scores = lax.dot_general(
                all_q[j], rec_ref[0, j, at, :], (((1,), (1,)), ((), ())),
                preferred_element_type=jnp.float32,
            )
            scores = jnp.where(place < lengths[j] - base, scores, DEAD)
            before = running[0, j]
            top = jnp.maximum(before, jnp.max(scores, axis=1, keepdims=True))
            weights = jnp.exp((scores - jnp.concatenate([top, top], axis=1)) * SCALE)
            shrink = jnp.exp((before - top) * SCALE)
            running[0, j] = top
            running[1, j] = running[1, j] * shrink + jnp.sum(weights, axis=1, keepdims=True)
            mail[0, j] = mail[0, j] * shrink + jnp.dot(
                weights.astype(jnp.bfloat16), rec_ref[1, j, at, :],
                preferred_element_type=jnp.float32,
            )

    arrived(first)
    attend(z)

    def recv_round(k, carry):
        for dz in (k, chips - k):
            arrived(partner(dz, False))
            arrived(partner(dz, True))
            attend(lax.rem(z + dz, chips))
        return carry

    lax.fori_loop(1, chips // 2, recv_round, 0)
    arrived(partner(chips // 2, False))
    arrived(partner(chips // 2, True))
    attend(lax.rem(z + chips // 2, chips))

    half = lax.broadcasted_iota(jnp.int32, mail.shape[1:], 2) < HD // 2
    mail[1] = jnp.where(half, running[0], running[1])
    for k in range(1, n_tp):
        mail_copy(tp, lax.rem(tp + k, n_tp)).start()
    box[tp] = mail[:, :, pl.ds(tp * rows, rows), :]
    for k in range(1, n_tp):
        t = lax.rem(tp + k, n_tp)
        mail_copy(t, t).wait_recv()

    for j in range(slots):
        tops, totals = [], []
        for t in range(n_tp):
            both = box[t, 1, j]
            tops.append(jnp.broadcast_to(both[:, 0:1], (rows, HD)))
            totals.append(jnp.broadcast_to(both[:, HD // 2 : HD // 2 + 1], (rows, HD)))
        tops.append(box[n_tp, 1, j])
        totals.append(running[2, j, 0:rows])
        top = tops[0]
        for other in tops[1:]:
            top = jnp.maximum(top, other)
        total = jnp.zeros((rows, HD), jnp.float32)
        summed = jnp.zeros((rows, HD), jnp.float32)
        for t in range(n_tp + 1):
            share = jnp.exp((tops[t] - top) * SCALE)
            total = total + totals[t] * share
            summed = summed + box[t, 0, j] * share
        out_ref[j] = (summed / total).astype(out_ref.dtype)

    def sent(k, carry):
        to(lax.rem(me + k, n_ctx)).wait_send()
        return carry

    lax.fori_loop(1, n_ctx, sent, 0)
    for k in range(1, n_tp):
        t = lax.rem(tp + k, n_tp)
        q_copy(tp, t).wait_send()
        mail_copy(tp, t).wait_send()


def shards(prefill_cache, lengths, slot_of, queries, new_kv):
    n_ctx, n_tp = lax.axis_size("ctx"), lax.axis_size("tp")
    _, requests, block, width = prefill_cache.shape
    slots = requests // n_ctx
    own_heads = queries.shape[2] // HD
    rows = STEPS * own_heads
    attended, received = pl.pallas_call(
        kernel,
        out_shape=(
            jax.ShapeDtypeStruct((slots, rows, HD), jnp.bfloat16),
            jax.ShapeDtypeStruct((2, slots, n_ctx * block, width), jnp.bfloat16),
        ),
        in_specs=[pl.BlockSpec(memory_space=pltpu.HBM)] * 5,
        out_specs=(
            pl.BlockSpec(memory_space=pltpu.VMEM),
            pl.BlockSpec(memory_space=pltpu.VMEM),
        ),
        scratch_shapes=[
            pltpu.SMEM(slot_of.shape, jnp.int32),
            pltpu.SMEM(lengths.shape, jnp.int32),
            pltpu.VMEM(queries.shape, jnp.bfloat16),
            pltpu.VMEM(new_kv.shape, jnp.bfloat16),
            pltpu.VMEM(prefill_cache.shape, jnp.bfloat16),
            pltpu.VMEM((n_ctx, 2, slots, block, width), jnp.bfloat16),
            pltpu.VMEM((slots, rows, HD), jnp.float32),
            pltpu.VMEM((slots, n_tp * rows, HD), jnp.bfloat16),
            pltpu.VMEM((2, slots, n_tp * rows, HD), jnp.float32),
            pltpu.VMEM((3, slots, n_tp * rows, HD), jnp.float32),
            pltpu.VMEM((n_tp + 1, 2, slots, rows, HD), jnp.float32),
            pltpu.SemaphoreType.DMA((5,)),
            pltpu.SemaphoreType.DMA((n_ctx,)),
            pltpu.SemaphoreType.DMA((n_ctx,)),
            pltpu.SemaphoreType.DMA((n_tp,)),
            pltpu.SemaphoreType.DMA((n_tp,)),
            pltpu.SemaphoreType.DMA((n_tp,)),
            pltpu.SemaphoreType.DMA((n_tp,)),
        ],
        compiler_params=pltpu.CompilerParams(
            collective_id=0, has_side_effects=True, vmem_limit_bytes=32 << 20
        ),
        name="handover",
    )(
        *(
            pltpu.with_memory_space_constraint(array, pltpu.HBM)
            for array in (prefill_cache, slot_of, lengths, queries, new_kv)
        )
    )
    attended = attended.reshape(slots, STEPS, own_heads * HD).transpose(1, 0, 2)
    return attended, received


def solution(mesh):
    return jax.shard_map(
        shards,
        mesh=mesh,
        in_specs=(
            P(None, None, ("ctx", "tp"), "kvh"),
            P(),
            P(),
            P(None, "ctx", ("kvh", "tp")),
            P(None, None, "ctx", "kvh"),
        ),
        out_specs=(P(None, "ctx", ("kvh", "tp")), P(None, "ctx", "tp", "kvh")),
        check_vma=False,
    )
```

```python
import math

import jax
import jax.numpy as jnp
from jax import lax
from jax.experimental import pallas as pl
from jax.experimental.pallas import tpu as pltpu
from jax.sharding import PartitionSpec as P

HD = 128
STEPS = 4
SCALE = 1.0 / math.sqrt(HD)
MESH = pl.DeviceIdType.MESH
DEAD = -1e38
FLOOR = -1e30

SEND_ORDER = (
    (1, 7, 4, 6, 5, 3, 2),
    (3, 1, 7, 4, 2, 6, 5),
    (1, 7, 4, 2, 6, 3, 5),
    (6, 1, 7, 2, 3, 5, 4),
    (1, 4, 5, 6, 2, 7, 3),
    (1, 7, 4, 2, 6, 3, 5),
    (1, 7, 5, 2, 6, 3, 4),
    (1, 7, 4, 6, 2, 3, 5),
)
RECV_ORDER = (
    (7, 4, 1, 6, 2, 3, 5),
    (7, 2, 1, 3, 4, 6, 5),
    (7, 1, 2, 5, 6, 3, 4),
    (7, 3, 4, 2, 6, 1, 5),
    (5, 1, 7, 4, 6, 2, 3),
    (7, 1, 2, 6, 4, 3, 5),
    (7, 1, 4, 2, 6, 5, 3),
    (7, 1, 6, 2, 3, 5, 4),
)


def by_chip(orders, z, radix):
    code = jnp.int32(0)
    for chip, order in enumerate(orders):
        number = sum(distance * radix**i for i, distance in enumerate(order))
        code = code + jnp.where(z == chip, number, 0)
    return code


def kernel(
    cache_in, slot_in, len_in, query_in, new_in,
    rec_ref, box,
    slot_ref, len_ref, query_ref, new_ref, raw, stage, own_q, all_q, mail, running,
    load_sem, send_sem, recv_sem, q_send_sem, q_recv_sem, mail_send_sem, mail_recv_sem, ready,
):
    me = lax.axis_index("ctx")
    tp = lax.axis_index("tp")
    z, core = me // 2, lax.rem(me, 2)
    n_ctx = lax.axis_size("ctx")
    n_tp = lax.axis_size("tp")
    chips = n_ctx // 2
    requests = slot_ref.shape[0]
    slots = requests // n_ctx
    block = raw.shape[2]
    own_heads = query_ref.shape[2] // HD
    rows = STEPS * own_heads

    loads = [
        pltpu.make_async_copy(source, target, load_sem.at[i])
        for i, (source, target) in enumerate(
            [(slot_in, slot_ref)]
            + [(cache_in.at[k, pl.ds(i * 8, 8)], raw.at[k, pl.ds(i * 8, 8)]) for k in range(2) for i in range(requests // 8)]
            + [(query_in, query_ref), (len_in, len_ref), (new_in, new_ref)]
        )
    ]
    for load in loads:
        load.start()

    barrier = pltpu.get_barrier_semaphore()
    for k in range(1, n_tp):
        pl.semaphore_signal(
            barrier, inc=1, device_id={"tp": lax.rem(tp + k, n_tp)}, device_id_type=MESH
        )
    for d in range(n_ctx):

        @pl.when((d // 2 >= z) & (d != me))
        def _():
            pl.semaphore_signal(barrier, inc=1, device_id={"ctx": d}, device_id_type=MESH)

    pl.semaphore_wait(barrier, 2 * z + 1 + n_tp - 1)
    for d in range(n_ctx - 2):

        @pl.when(d // 2 < z)
        def _():
            pl.semaphore_signal(ready.at[me], inc=1, device_id={"ctx": d}, device_id_type=MESH)

    def request_of(slot):
        found = jnp.int32(0)
        for r in range(1, requests):
            found = jnp.where(slot_ref[r] == slot, r, found)
        return found

    def fill(d):
        for j in range(slots):
            r = request_of(d * slots + j)
            for k in range(2):
                stage[d, k, j] = raw[k, r]

    def to(d):
        return pltpu.make_async_remote_copy(
            src_ref=stage.at[d],
            dst_ref=rec_ref.at[:, :, pl.ds(me * block, block)],
            send_sem=send_sem.at[d],
            recv_sem=recv_sem.at[me],
            device_id={"ctx": d},
            device_id_type=MESH,
        )

    def arrived(d):
        pltpu.make_async_remote_copy(
            src_ref=stage.at[d],
            dst_ref=rec_ref.at[:, :, pl.ds(d * block, block)],
            send_sem=send_sem.at[d],
            recv_sem=recv_sem.at[d],
            device_id={"ctx": d},
            device_id_type=MESH,
        ).wait_recv()

    def q_copy(owner, t):
        here = all_q.at[:, pl.ds(owner * rows, rows)]
        return pltpu.make_async_remote_copy(
            src_ref=here, dst_ref=here,
            send_sem=q_send_sem.at[t], recv_sem=q_recv_sem.at[owner],
            device_id={"tp": t}, device_id_type=MESH,
        )

    def mail_copy(owner, t):
        return pltpu.make_async_remote_copy(
            src_ref=mail.at[:, :, pl.ds(t * rows, rows)], dst_ref=box.at[owner],
            send_sem=mail_send_sem.at[t], recv_sem=mail_recv_sem.at[owner],
            device_id={"tp": t}, device_id_type=MESH,
        )

    for load in loads:
        load.wait()

    def serve(i, code):
        chip = lax.rem(z + lax.rem(code, chips), chips)
        for other in range(2):
            d = chip * 2 + lax.rem(core + other, 2)

            @pl.when(chip > z)
            def _():
                pl.semaphore_wait(ready.at[d], 1)

            fill(d)
            to(d).start()
        return code // chips

    send_code = by_chip(SEND_ORDER, z, chips)
    twin = z * 2 + 1 - core
    lax.fori_loop(0, chips - 1, serve, send_code)
    fill(twin)
    to(twin).start()

    for j in range(slots):
        for s in range(STEPS):
            for h in range(own_heads):
                own_q[j, s * own_heads + h, :] = query_ref[
                    s, j, h * HD : (h + 1) * HD
                ].astype(jnp.float32)
    all_q[:, pl.ds(tp * rows, rows), :] = own_q[...].astype(jnp.bfloat16)
    for k in range(1, n_tp):
        q_copy(tp, lax.rem(tp + k, n_tp)).start()

    fill(me)
    rec_ref[:, :, pl.ds(me * block, block), :] = stage[me]

    def packed(top, total):
        lanes = lax.broadcasted_iota(jnp.int32, top.shape, len(top.shape) - 1)
        return jnp.where(lanes < HD // 2, top, total)

    row_step = lax.broadcasted_iota(jnp.int32, (rows, HD), 0) // own_heads
    for j in range(slots):
        queries = own_q[j]
        scores = []
        for u in range(STEPS):
            key = new_ref[0, u, j, :].astype(jnp.float32).reshape(1, HD)
            dots = jnp.sum(queries * key, axis=1, keepdims=True)
            scores.append(jnp.where(row_step >= u, jnp.broadcast_to(dots, (rows, HD)), DEAD))
        top = scores[0]
        for u in range(1, STEPS):
            top = jnp.maximum(top, scores[u])
        total = jnp.zeros((rows, HD), jnp.float32)
        summed = jnp.zeros((rows, HD), jnp.float32)
        for u in range(STEPS):
            weight = jnp.exp((scores[u] - top) * SCALE)
            value = new_ref[1, u, j, :].astype(jnp.float32).reshape(1, HD)
            total = total + weight
            summed = summed + weight.astype(jnp.bfloat16).astype(jnp.float32) * value
        box[n_tp, 0, j] = summed
        box[n_tp, 1, j] = packed(top, total)

    lengths = [len_ref[request_of(me * slots + j)] for j in range(slots)]
    mail[0] = jnp.zeros(mail.shape[1:], jnp.float32)
    running[0] = jnp.full(running.shape[1:], FLOOR, jnp.float32)
    running[1] = jnp.zeros(running.shape[1:], jnp.float32)

    for k in range(1, n_tp):
        t = lax.rem(tp + k, n_tp)
        q_copy(t, t).wait_recv()

    span = 2 * block
    lane = lax.broadcasted_iota(jnp.int32, (n_tp * rows, span), 1)
    place = (lane // block) * (n_tp * block) + lax.rem(lane, block)

    def attend(chip):
        at = pl.ds(pl.multiple_of(chip * span, span), span)
        base = (chip * 2 * n_tp + tp) * block
        for j in range(slots):
            scores = lax.dot_general(
                all_q[j], rec_ref[0, j, at, :], (((1,), (1,)), ((), ())),
                preferred_element_type=jnp.float32,
            )
            scores = jnp.where(place < lengths[j] - base, scores, DEAD)
            before = running[0, j]
            top = jnp.maximum(before, jnp.max(scores, axis=1, keepdims=True))
            weights = jnp.exp((scores - jnp.concatenate([top, top], axis=1)) * SCALE)
            shrink = jnp.exp((before - top) * SCALE)
            running[0, j] = top
            running[1, j] = running[1, j] * shrink + jnp.sum(weights, axis=1, keepdims=True)
            mail[0, j] = mail[0, j] * shrink + jnp.dot(
                weights.astype(jnp.bfloat16), rec_ref[1, j, at, :],
                preferred_element_type=jnp.float32,
            )

    arrived(twin)
    attend(z)

    def collect(i, code):
        chip = lax.rem(z + lax.rem(code, chips), chips)
        arrived(chip * 2 + core)
        arrived(chip * 2 + 1 - core)
        attend(chip)
        return code // chips

    recv_code = by_chip(RECV_ORDER, z, chips)
    lax.fori_loop(0, chips - 1, collect, recv_code)

    mail[1] = packed(running[0], running[1])
    for k in range(1, n_tp):
        mail_copy(tp, lax.rem(tp + k, n_tp)).start()
    box[tp] = mail[:, :, pl.ds(tp * rows, rows), :]

    def sent(k, carry):
        to(lax.rem(me + k, n_ctx)).wait_send()
        return carry

    lax.fori_loop(1, n_ctx, sent, 0)
    for k in range(1, n_tp):
        q_copy(tp, lax.rem(tp + k, n_tp)).wait_send()
    for k in range(1, n_tp):
        t = lax.rem(tp + k, n_tp)
        mail_copy(t, t).wait_recv()
        mail_copy(tp, t).wait_send()


def finish(rec_ref, box, out_ref, cache_ref, held, sem):
    copies = [
        pltpu.make_async_copy(rec_ref.at[k, j], cache_ref.at[k, j], sem.at[k, j])
        for k in range(rec_ref.shape[0])
        for j in range(rec_ref.shape[1])
    ]
    for copy in copies:
        copy.start()
    parts, _, slots, rows, _ = box.shape
    own_heads = rows // STEPS
    results = []
    for j in range(slots):
        tops, totals = [], []
        for t in range(parts):
            both = box[t, 1, j]
            tops.append(jnp.broadcast_to(both[:, 0:1], (rows, HD)))
            totals.append(jnp.broadcast_to(both[:, HD // 2 : HD // 2 + 1], (rows, HD)))
        top = tops[0]
        for other in tops[1:]:
            top = jnp.maximum(top, other)
        total = jnp.zeros((rows, HD), jnp.float32)
        summed = jnp.zeros((rows, HD), jnp.float32)
        for t in range(parts):
            share = jnp.exp((tops[t] - top) * SCALE)
            total = total + totals[t] * share
            summed = summed + box[t, 0, j] * share
        results.append(summed / total)
    for s in range(STEPS):
        for h in range(own_heads):
            r = s * own_heads + h
            piece = jnp.concatenate([result[r : r + 1] for result in results], axis=0)
            held[s, :, h * HD : (h + 1) * HD] = piece.astype(held.dtype)
    last = pltpu.make_async_copy(held, out_ref, sem.at[0, slots])
    last.start()
    last.wait()
    for copy in copies:
        copy.wait()


def shards(prefill_cache, lengths, slot_of, queries, new_kv):
    n_ctx, n_tp = lax.axis_size("ctx"), lax.axis_size("tp")
    _, requests, block, width = prefill_cache.shape
    slots = requests // n_ctx
    own_heads = queries.shape[2] // HD
    rows = STEPS * own_heads
    operands = (prefill_cache, slot_of, lengths, queries, new_kv)
    received, box = pl.pallas_call(
        kernel,
        out_shape=(
            jax.ShapeDtypeStruct((2, slots, n_ctx * block, width), jnp.bfloat16),
            jax.ShapeDtypeStruct((n_tp + 1, 2, slots, rows, HD), jnp.float32),
        ),
        in_specs=[pl.BlockSpec(memory_space=pltpu.HBM)] * len(operands),
        out_specs=(
            pl.BlockSpec(memory_space=pltpu.VMEM),
            pl.BlockSpec(memory_space=pltpu.VMEM),
        ),
        scratch_shapes=[
            pltpu.SMEM(slot_of.shape, jnp.int32),
            pltpu.SMEM(lengths.shape, jnp.int32),
            pltpu.VMEM(queries.shape, jnp.bfloat16),
            pltpu.VMEM(new_kv.shape, jnp.bfloat16),
            pltpu.VMEM(prefill_cache.shape, jnp.bfloat16),
            pltpu.VMEM((n_ctx, 2, slots, block, width), jnp.bfloat16),
            pltpu.VMEM((slots, rows, HD), jnp.float32),
            pltpu.VMEM((slots, n_tp * rows, HD), jnp.bfloat16),
            pltpu.VMEM((2, slots, n_tp * rows, HD), jnp.float32),
            pltpu.VMEM((2, slots, n_tp * rows, HD), jnp.float32),
            pltpu.SemaphoreType.DMA((4 + 2 * (requests // 8),)),
            pltpu.SemaphoreType.DMA((n_ctx,)),
            pltpu.SemaphoreType.DMA((n_ctx,)),
            pltpu.SemaphoreType.DMA((n_tp,)),
            pltpu.SemaphoreType.DMA((n_tp,)),
            pltpu.SemaphoreType.DMA((n_tp,)),
            pltpu.SemaphoreType.DMA((n_tp,)),
            pltpu.SemaphoreType.REGULAR((n_ctx,)),
        ],
        compiler_params=pltpu.CompilerParams(
            collective_id=0, has_side_effects=True, vmem_limit_bytes=32 << 20
        ),
        name="handover",
    )(*(pltpu.with_memory_space_constraint(operand, pltpu.HBM) for operand in operands))
    return pl.pallas_call(
        finish,
        out_shape=(
            jax.ShapeDtypeStruct(queries.shape, jnp.bfloat16),
            jax.ShapeDtypeStruct(received.shape, jnp.bfloat16),
        ),
        in_specs=[pl.BlockSpec(memory_space=pltpu.VMEM)] * 2,
        out_specs=(pl.BlockSpec(memory_space=pltpu.HBM), pl.BlockSpec(memory_space=pltpu.HBM)),
        scratch_shapes=[
            pltpu.VMEM(queries.shape, jnp.bfloat16),
            pltpu.SemaphoreType.DMA((2, slots + 1)),
        ],
        compiler_params=pltpu.CompilerParams(vmem_limit_bytes=16 << 20),
        name="finish",
    )(received, box)


def solution(mesh):
    return jax.shard_map(
        shards,
        mesh=mesh,
        in_specs=(
            P(None, None, ("ctx", "tp"), "kvh"),
            P(),
            P(),
            P(None, "ctx", ("kvh", "tp")),
            P(None, None, "ctx", "kvh"),
        ),
        out_specs=(P(None, "ctx", ("kvh", "tp")), P(None, "ctx", "tp", "kvh")),
        check_vma=False,
    )
```

```python
import math

import jax
import jax.numpy as jnp
from jax import lax
from jax.experimental import pallas as pl
from jax.experimental.pallas import tpu as pltpu
from jax.sharding import PartitionSpec as P

HD = 128
STEPS = 4
SCALE = 1.0 / math.sqrt(HD)
MESH = pl.DeviceIdType.MESH
DEAD = -1e38
FLOOR = -1e30

SEND_ORDER = (
    (3, 5, 2, 7, 1, 4, 6),
    (2, 1, 4, 7, 6, 5, 3),
    (1, 3, 7, 6, 2, 4, 5),
    (5, 1, 2, 3, 6, 7, 4),
    (5, 4, 2, 6, 7, 1, 3),
    (3, 4, 7, 1, 5, 2, 6),
    (6, 2, 5, 3, 1, 4, 7),
    (1, 5, 4, 2, 6, 7, 3),
)
HOLDER, VIA, GOAL, TURN = 4, 3, 0, 4
RECV_ORDER = (
    (1, 5, 3, 6, 4, 7, 2),
    (4, 3, 7, 1, 5, 2, 6),
    (6, 2, 7, 1, 5, 3, 4),
    (5, 7, 6, 4, 3, 2, 1),
    (7, 1, 3, 4, 2, 5, 6),
    (4, 6, 3, 5, 7, 2, 1),
    (6, 7, 3, 2, 4, 1, 5),
    (2, 1, 6, 5, 7, 3, 4),
)


def by_chip(orders, z, radix):
    code = jnp.int32(0)
    for chip, order in enumerate(orders):
        number = sum(distance * radix**i for i, distance in enumerate(order))
        code = code + jnp.where(z == chip, number, 0)
    return code


def kernel(
    cache_in, slot_in, len_in, query_in, new_in,
    rec_ref, box,
    slot_ref, len_ref, query_ref, new_ref, raw, stage, passing, own_q, all_q, mail, running,
    load_sem, send_sem, recv_sem, q_send_sem, q_recv_sem, mail_send_sem, mail_recv_sem, pass_sem, ready,
):
    me = lax.axis_index("ctx")
    tp = lax.axis_index("tp")
    z, core = me // 2, lax.rem(me, 2)
    n_ctx = lax.axis_size("ctx")
    n_tp = lax.axis_size("tp")
    chips = n_ctx // 2
    requests = slot_ref.shape[0]
    slots = requests // n_ctx
    block = raw.shape[2]
    own_heads = query_ref.shape[2] // HD
    rows = STEPS * own_heads

    loads = [
        pltpu.make_async_copy(source, target, load_sem.at[i])
        for i, (source, target) in enumerate(
            [(slot_in, slot_ref)]
            + [(cache_in.at[k, pl.ds(i * 8, 8)], raw.at[k, pl.ds(i * 8, 8)]) for k in range(2) for i in range(requests // 8)]
            + [(query_in, query_ref), (len_in, len_ref), (new_in, new_ref)]
        )
    ]
    for load in loads:
        load.start()

    barrier = pltpu.get_barrier_semaphore()
    for k in range(1, n_tp):
        pl.semaphore_signal(
            barrier, inc=1, device_id={"tp": lax.rem(tp + k, n_tp)}, device_id_type=MESH
        )
    for d in range(n_ctx):

        @pl.when((d // 2 >= z) & (d != me))
        def _():
            pl.semaphore_signal(barrier, inc=1, device_id={"ctx": d}, device_id_type=MESH)

    pl.semaphore_wait(barrier, 2 * z + 1 + n_tp - 1)
    for d in range(n_ctx - 2):

        @pl.when(d // 2 < z)
        def _():
            pl.semaphore_signal(ready.at[me], inc=1, device_id={"ctx": d}, device_id_type=MESH)

    def request_of(slot):
        found = jnp.int32(0)
        for r in range(1, requests):
            found = jnp.where(slot_ref[r] == slot, r, found)
        return found

    def fill(d, found):
        for j in range(slots):
            for k in range(2):
                stage[d, k, j] = raw[k, found[j]]

    def to(d):
        return pltpu.make_async_remote_copy(
            src_ref=stage.at[d],
            dst_ref=rec_ref.at[:, :, pl.ds(me * block, block)],
            send_sem=send_sem.at[d],
            recv_sem=recv_sem.at[me],
            device_id={"ctx": d},
            device_id_type=MESH,
        )

    def to_via(d):
        return pltpu.make_async_remote_copy(
            src_ref=stage.at[d],
            dst_ref=passing,
            send_sem=send_sem.at[d],
            recv_sem=pass_sem.at[0],
            device_id={"ctx": VIA * 2 + core},
            device_id_type=MESH,
        )

    def pass_on():
        source = HOLDER * 2 + core
        return pltpu.make_async_remote_copy(
            src_ref=passing,
            dst_ref=rec_ref.at[:, :, pl.ds(source * block, block)],
            send_sem=pass_sem.at[1],
            recv_sem=recv_sem.at[source],
            device_id={"ctx": GOAL * 2 + 1 - core},
            device_id_type=MESH,
        )

    def arrived(d):
        pltpu.make_async_remote_copy(
            src_ref=stage.at[d],
            dst_ref=rec_ref.at[:, :, pl.ds(d * block, block)],
            send_sem=send_sem.at[d],
            recv_sem=recv_sem.at[d],
            device_id={"ctx": d},
            device_id_type=MESH,
        ).wait_recv()

    def q_copy(owner, t):
        here = all_q.at[:, pl.ds(owner * rows, rows)]
        return pltpu.make_async_remote_copy(
            src_ref=here, dst_ref=here,
            send_sem=q_send_sem.at[t], recv_sem=q_recv_sem.at[owner],
            device_id={"tp": t}, device_id_type=MESH,
        )

    def mail_copy(owner, t):
        return pltpu.make_async_remote_copy(
            src_ref=mail.at[:, pl.ds(t * rows, rows)], dst_ref=box.at[owner],
            send_sem=mail_send_sem.at[t], recv_sem=mail_recv_sem.at[owner],
            device_id={"tp": t}, device_id_type=MESH,
        )

    def serve(i, carry):
        code, now = carry

        @pl.when((z == VIA) & (i == TURN))
        def _():
            to_via(GOAL * 2 + 1 - core).wait_recv()
            pass_on().start()

        chip = lax.rem(z + lax.rem(code, chips), chips)
        for other in range(2):
            d = chip * 2 + lax.rem(core + other, 2)

            @pl.when(chip > z)
            def _():
                pl.semaphore_wait(ready.at[d], 1)

            fill(d, now[other * slots : (other + 1) * slots])
            if other == 0:
                to(d).start()
            else:
                around = (z == HOLDER) & (chip == GOAL)

                @pl.when(around)
                def _():
                    to_via(d).start()

                @pl.when(jnp.logical_not(around))
                def _():
                    to(d).start()

        return code // chips, requests_of(code // chips)

    def requests_of(code):
        chip = lax.rem(z + lax.rem(code, chips), chips)
        return tuple(
            request_of((chip * 2 + lax.rem(core + other, 2)) * slots + j)
            for other in range(2)
            for j in range(slots)
        )

    send_code = by_chip(SEND_ORDER, z, chips)
    twin = z * 2 + 1 - core
    loads[0].wait()
    first = requests_of(send_code)
    for load in loads[1:-3]:
        load.wait()
    lax.fori_loop(0, chips - 1, serve, (send_code, first))
    fill(twin, [request_of(twin * slots + j) for j in range(slots)])
    to(twin).start()
    for load in loads[-3:]:
        load.wait()

    for j in range(slots):
        for s in range(STEPS):
            for h in range(own_heads):
                own_q[j, s * own_heads + h, :] = query_ref[
                    s, j, h * HD : (h + 1) * HD
                ].astype(jnp.float32)
    all_q[:, pl.ds(tp * rows, rows), :] = own_q[...].astype(jnp.bfloat16)
    for k in range(1, n_tp):
        q_copy(tp, lax.rem(tp + k, n_tp)).start()

    own = [request_of(me * slots + j) for j in range(slots)]
    for j in range(slots):
        for k in range(2):
            rec_ref[k, j, pl.ds(me * block, block), :] = raw[k, own[j]]

    def packed(tops, totals):
        bands = [both[j] for j in range(slots) for both in (tops, totals)]
        band = lax.broadcasted_iota(jnp.int32, bands[0].shape, 1) // (HD // len(bands))
        result = bands[0]
        for i in range(1, len(bands)):
            result = jnp.where(band == i, bands[i], result)
        return result

    new_tops, new_totals = [], []
    row_step = lax.broadcasted_iota(jnp.int32, (rows, HD), 0) // own_heads
    for j in range(slots):
        queries = own_q[j]
        scores = []
        for u in range(STEPS):
            key = new_ref[0, u, j, :].astype(jnp.float32).reshape(1, HD)
            dots = jnp.sum(queries * key, axis=1, keepdims=True)
            scores.append(jnp.where(row_step >= u, jnp.broadcast_to(dots, (rows, HD)), DEAD))
        top = scores[0]
        for u in range(1, STEPS):
            top = jnp.maximum(top, scores[u])
        total = jnp.zeros((rows, HD), jnp.float32)
        summed = jnp.zeros((rows, HD), jnp.float32)
        for u in range(STEPS):
            weight = jnp.exp((scores[u] - top) * SCALE)
            value = new_ref[1, u, j, :].astype(jnp.float32).reshape(1, HD)
            total = total + weight
            summed = summed + weight.astype(jnp.bfloat16).astype(jnp.float32) * value
        box[n_tp, j] = summed
        new_tops.append(top)
        new_totals.append(total)
    box[n_tp, slots] = packed(new_tops, new_totals)

    lengths = [len_ref[r] for r in own]
    mail[...] = jnp.zeros(mail.shape, jnp.float32)
    running[0] = jnp.full(running.shape[1:], FLOOR, jnp.float32)
    running[1] = jnp.zeros(running.shape[1:], jnp.float32)

    for k in range(1, n_tp):
        t = lax.rem(tp + k, n_tp)
        q_copy(t, t).wait_recv()

    span = 2 * block
    lane = lax.broadcasted_iota(jnp.int32, (n_tp * rows, span), 1)
    place = (lane // block) * (n_tp * block) + lax.rem(lane, block)

    def attend(chip):
        at = pl.ds(pl.multiple_of(chip * span, span), span)
        base = (chip * 2 * n_tp + tp) * block
        each = range(slots)
        scores = [
            lax.dot_general(
                all_q[j], rec_ref[0, j, at, :], (((1,), (1,)), ((), ())),
                preferred_element_type=jnp.float32,
            )
            for j in each
        ]
        scores = [jnp.where(place < lengths[j] - base, scores[j], DEAD) for j in each]
        before = [running[0, j] for j in each]
        top = [jnp.maximum(before[j], jnp.max(scores[j], axis=1, keepdims=True)) for j in each]
        weights = [
            jnp.exp((scores[j] - jnp.concatenate([top[j], top[j]], axis=1)) * SCALE) for j in each
        ]
        summed = [
            jnp.dot(
                weights[j].astype(jnp.bfloat16), rec_ref[1, j, at, :],
                preferred_element_type=jnp.float32,
            )
            for j in each
        ]
        shrink = [jnp.exp((before[j] - top[j]) * SCALE) for j in each]
        totals = [
            running[1, j] * shrink[j] + jnp.sum(weights[j], axis=1, keepdims=True) for j in each
        ]
        summed = [mail[j] * shrink[j] + summed[j] for j in each]
        for j in each:
            running[0, j] = top[j]
            running[1, j] = totals[j]
            mail[j] = summed[j]

    arrived(twin)
    attend(z)

    def collect(i, code):
        chip = lax.rem(z + lax.rem(code, chips), chips)
        arrived(chip * 2 + core)
        arrived(chip * 2 + 1 - core)
        attend(chip)
        return code // chips

    recv_code = by_chip(RECV_ORDER, z, chips)
    lax.fori_loop(0, chips - 1, collect, recv_code)

    mail[slots] = packed([running[0, j] for j in range(slots)], [running[1, j] for j in range(slots)])
    for k in range(1, n_tp):
        mail_copy(tp, lax.rem(tp + k, n_tp)).start()
    box[tp] = mail[:, pl.ds(tp * rows, rows), :]

    def sent(k, carry):
        to(lax.rem(me + k, n_ctx)).wait_send()
        return carry

    lax.fori_loop(1, n_ctx, sent, 0)

    @pl.when(z == VIA)
    def _():
        pass_on().wait_send()

    for k in range(1, n_tp):
        q_copy(tp, lax.rem(tp + k, n_tp)).wait_send()
    for k in range(1, n_tp):
        t = lax.rem(tp + k, n_tp)
        mail_copy(t, t).wait_recv()
        mail_copy(tp, t).wait_send()


def finish(rec_ref, box, out_ref, cache_ref, held, sem):
    copies = [
        pltpu.make_async_copy(rec_ref.at[k, j], cache_ref.at[k, j], sem.at[k, j])
        for k in range(rec_ref.shape[0])
        for j in range(rec_ref.shape[1])
    ]
    for copy in copies:
        copy.start()
    parts, rows = box.shape[0], box.shape[2]
    slots = box.shape[1] - 1
    band = HD // (2 * slots)
    own_heads = rows // STEPS
    results = []
    for j in range(slots):
        tops, totals = [], []
        for t in range(parts):
            bands = box[t, slots]
            at = 2 * j * band
            tops.append(jnp.broadcast_to(bands[:, at : at + 1], (rows, HD)))
            totals.append(jnp.broadcast_to(bands[:, at + band : at + band + 1], (rows, HD)))
        top = tops[0]
        for other in tops[1:]:
            top = jnp.maximum(top, other)
        total = jnp.zeros((rows, HD), jnp.float32)
        summed = jnp.zeros((rows, HD), jnp.float32)
        for t in range(parts):
            share = jnp.exp((tops[t] - top) * SCALE)
            total = total + totals[t] * share
            summed = summed + box[t, j] * share
        results.append(summed / total)
    for s in range(STEPS):
        for h in range(own_heads):
            r = s * own_heads + h
            piece = jnp.concatenate([result[r : r + 1] for result in results], axis=0)
            held[s, :, h * HD : (h + 1) * HD] = piece.astype(held.dtype)
    last = pltpu.make_async_copy(held, out_ref, sem.at[0, slots])
    last.start()
    last.wait()
    for copy in copies:
        copy.wait()


def shards(prefill_cache, lengths, slot_of, queries, new_kv):
    n_ctx, n_tp = lax.axis_size("ctx"), lax.axis_size("tp")
    _, requests, block, width = prefill_cache.shape
    slots = requests // n_ctx
    own_heads = queries.shape[2] // HD
    rows = STEPS * own_heads
    operands = (prefill_cache, slot_of, lengths, queries, new_kv)
    received, box = pl.pallas_call(
        kernel,
        out_shape=(
            jax.ShapeDtypeStruct((2, slots, n_ctx * block, width), jnp.bfloat16),
            jax.ShapeDtypeStruct((n_tp + 1, slots + 1, rows, HD), jnp.float32),
        ),
        in_specs=[pl.BlockSpec(memory_space=pltpu.HBM)] * len(operands),
        out_specs=(
            pl.BlockSpec(memory_space=pltpu.VMEM),
            pl.BlockSpec(memory_space=pltpu.VMEM),
        ),
        scratch_shapes=[
            pltpu.SMEM(slot_of.shape, jnp.int32),
            pltpu.SMEM(lengths.shape, jnp.int32),
            pltpu.VMEM(queries.shape, jnp.bfloat16),
            pltpu.VMEM(new_kv.shape, jnp.bfloat16),
            pltpu.VMEM(prefill_cache.shape, jnp.bfloat16),
            pltpu.VMEM((n_ctx, 2, slots, block, width), jnp.bfloat16),
            pltpu.VMEM((2, slots, block, width), jnp.bfloat16),
            pltpu.VMEM((slots, rows, HD), jnp.float32),
            pltpu.VMEM((slots, n_tp * rows, HD), jnp.bfloat16),
            pltpu.VMEM((slots + 1, n_tp * rows, HD), jnp.float32),
            pltpu.VMEM((2, slots, n_tp * rows, HD), jnp.float32),
            pltpu.SemaphoreType.DMA((4 + 2 * (requests // 8),)),
            pltpu.SemaphoreType.DMA((n_ctx,)),
            pltpu.SemaphoreType.DMA((n_ctx,)),
            pltpu.SemaphoreType.DMA((n_tp,)),
            pltpu.SemaphoreType.DMA((n_tp,)),
            pltpu.SemaphoreType.DMA((n_tp,)),
            pltpu.SemaphoreType.DMA((n_tp,)),
            pltpu.SemaphoreType.DMA((2,)),
            pltpu.SemaphoreType.REGULAR((n_ctx,)),
        ],
        compiler_params=pltpu.CompilerParams(
            collective_id=0, has_side_effects=True, vmem_limit_bytes=32 << 20
        ),
        name="handover",
    )(*(pltpu.with_memory_space_constraint(operand, pltpu.HBM) for operand in operands))
    return pl.pallas_call(
        finish,
        out_shape=(
            jax.ShapeDtypeStruct(queries.shape, jnp.bfloat16),
            jax.ShapeDtypeStruct(received.shape, jnp.bfloat16),
        ),
        in_specs=[pl.BlockSpec(memory_space=pltpu.VMEM)] * 2,
        out_specs=(pl.BlockSpec(memory_space=pltpu.HBM), pl.BlockSpec(memory_space=pltpu.HBM)),
        scratch_shapes=[
            pltpu.VMEM(queries.shape, jnp.bfloat16),
            pltpu.SemaphoreType.DMA((2, slots + 1)),
        ],
        compiler_params=pltpu.CompilerParams(vmem_limit_bytes=16 << 20),
        name="finish",
    )(received, box)


def solution(mesh):
    return jax.shard_map(
        shards,
        mesh=mesh,
        in_specs=(
            P(None, None, ("ctx", "tp"), "kvh"),
            P(),
            P(),
            P(None, "ctx", ("kvh", "tp")),
            P(None, None, "ctx", "kvh"),
        ),
        out_specs=(P(None, "ctx", ("kvh", "tp")), P(None, "ctx", "tp", "kvh")),
        check_vma=False,
    )
```

```python
import math

import jax
import jax.numpy as jnp
from jax import lax
from jax.experimental import pallas as pl
from jax.experimental.pallas import tpu as pltpu
from jax.sharding import PartitionSpec as P

HD = 128
STEPS = 4
SCALE = 1.0 / math.sqrt(HD)
MESH = pl.DeviceIdType.MESH
DEAD = -1e38
FLOOR = -1e30

SEND_ORDER = (
    (3, 5, 2, 7, 1, 4, 6),
    (2, 1, 4, 7, 6, 5, 3),
    (1, 3, 7, 6, 2, 4, 5),
    (5, 1, 2, 3, 6, 7, 4),
    (5, 4, 2, 6, 7, 1, 3),
    (3, 4, 7, 1, 5, 2, 6),
    (6, 2, 5, 3, 1, 4, 7),
    (1, 5, 4, 2, 6, 7, 3),
)
HOLDER, VIA, GOAL, TURN = 4, 3, 0, 4
RECV_ORDER = (
    (1, 5, 3, 6, 4, 7, 2),
    (4, 3, 7, 1, 5, 2, 6),
    (6, 2, 7, 1, 5, 3, 4),
    (5, 7, 6, 4, 3, 2, 1),
    (7, 1, 3, 4, 2, 5, 6),
    (4, 6, 3, 5, 7, 2, 1),
    (6, 7, 3, 2, 4, 1, 5),
    (2, 1, 6, 5, 7, 3, 4),
)


def by_chip(orders, z, radix):
    code = jnp.int32(0)
    for chip, order in enumerate(orders):
        number = sum(distance * radix**i for i, distance in enumerate(order))
        code = code + jnp.where(z == chip, number, 0)
    return code


def kernel(
    cache_in, slot_in, len_in, query_in, new_in,
    rec_ref, box,
    slot_ref, len_ref, query_ref, new_ref, raw_keys, raw_values, stage, passing, own_q, all_q, mail, running,
    load_sem, send_sem, recv_sem, q_send_sem, q_recv_sem, mail_send_sem, mail_recv_sem, pass_sem, ready,
):
    me = lax.axis_index("ctx")
    tp = lax.axis_index("tp")
    z, core = me // 2, lax.rem(me, 2)
    n_ctx = lax.axis_size("ctx")
    n_tp = lax.axis_size("tp")
    chips = n_ctx // 2
    requests = slot_ref.shape[0]
    slots = requests // n_ctx
    block = raw_keys.shape[1]
    raw = (raw_keys, raw_values)
    own_heads = query_ref.shape[2] // HD
    rows = STEPS * own_heads

    loads = [
        pltpu.make_async_copy(source, target, load_sem.at[i])
        for i, (source, target) in enumerate(
            [(slot_in, slot_ref)]
            + [(cache_in.at[k, pl.ds(i * 8, 8)], raw[k].at[pl.ds(i * 8, 8)]) for k in range(2) for i in range(requests // 8)]
            + [(query_in, query_ref), (len_in, len_ref), (new_in, new_ref)]
        )
    ]
    for load in loads:
        load.start()

    barrier = pltpu.get_barrier_semaphore()
    for k in range(1, n_tp):
        pl.semaphore_signal(
            barrier, inc=1, device_id={"tp": lax.rem(tp + k, n_tp)}, device_id_type=MESH
        )
    for d in range(n_ctx):

        @pl.when((d // 2 >= z) & (d != me))
        def _():
            pl.semaphore_signal(barrier, inc=1, device_id={"ctx": d}, device_id_type=MESH)

    pl.semaphore_wait(barrier, 2 * z + 1 + n_tp - 1)
    for d in range(n_ctx - 2):

        @pl.when(d // 2 < z)
        def _():
            pl.semaphore_signal(ready.at[me], inc=1, device_id={"ctx": d}, device_id_type=MESH)

    def request_of(slot):
        found = jnp.int32(0)
        for r in range(1, requests):
            found = jnp.where(slot_ref[r] == slot, r, found)
        return found

    def fill(d, found, kinds=range(2)):
        for j in range(slots):
            for k in kinds:
                stage[d, k, j] = raw[k][found[j]]

    def to(d):
        return pltpu.make_async_remote_copy(
            src_ref=stage.at[d],
            dst_ref=rec_ref.at[:, :, pl.ds(me * block, block)],
            send_sem=send_sem.at[d],
            recv_sem=recv_sem.at[me],
            device_id={"ctx": d},
            device_id_type=MESH,
        )

    def part_to(d, k):
        return pltpu.make_async_remote_copy(
            src_ref=stage.at[d, k],
            dst_ref=rec_ref.at[k, :, pl.ds(me * block, block)],
            send_sem=send_sem.at[d],
            recv_sem=recv_sem.at[me],
            device_id={"ctx": d},
            device_id_type=MESH,
        )

    def to_via(d):
        return pltpu.make_async_remote_copy(
            src_ref=stage.at[d],
            dst_ref=passing,
            send_sem=send_sem.at[d],
            recv_sem=pass_sem.at[0],
            device_id={"ctx": VIA * 2 + core},
            device_id_type=MESH,
        )

    def pass_on():
        source = HOLDER * 2 + core
        return pltpu.make_async_remote_copy(
            src_ref=passing,
            dst_ref=rec_ref.at[:, :, pl.ds(source * block, block)],
            send_sem=pass_sem.at[1],
            recv_sem=recv_sem.at[source],
            device_id={"ctx": GOAL * 2 + 1 - core},
            device_id_type=MESH,
        )

    def arrived(d):
        pltpu.make_async_remote_copy(
            src_ref=stage.at[d],
            dst_ref=rec_ref.at[:, :, pl.ds(d * block, block)],
            send_sem=send_sem.at[d],
            recv_sem=recv_sem.at[d],
            device_id={"ctx": d},
            device_id_type=MESH,
        ).wait_recv()

    def q_copy(owner, t):
        here = all_q.at[:, pl.ds(owner * rows, rows)]
        return pltpu.make_async_remote_copy(
            src_ref=here, dst_ref=here,
            send_sem=q_send_sem.at[t], recv_sem=q_recv_sem.at[owner],
            device_id={"tp": t}, device_id_type=MESH,
        )

    def mail_copy(owner, t):
        return pltpu.make_async_remote_copy(
            src_ref=mail.at[:, pl.ds(t * rows, rows)], dst_ref=box.at[owner],
            send_sem=mail_send_sem.at[t], recv_sem=mail_recv_sem.at[owner],
            device_id={"tp": t}, device_id_type=MESH,
        )

    def serve(i, carry):
        code, now = carry

        @pl.when((z == VIA) & (i == TURN))
        def _():
            to_via(GOAL * 2 + 1 - core).wait_recv()
            pass_on().start()

        chip = lax.rem(z + lax.rem(code, chips), chips)
        for other in range(2):
            d = chip * 2 + lax.rem(core + other, 2)

            @pl.when(chip > z)
            def _():
                pl.semaphore_wait(ready.at[d], 1)

            found = now[other * slots : (other + 1) * slots]
            if other == 0:
                fill(d, found, [0])
                part_to(d, 0).start()

                @pl.when(i == 0)
                def _():
                    for load in value_loads:
                        load.wait()

                fill(d, found, [1])
                part_to(d, 1).start()
            else:
                fill(d, found)
                around = (z == HOLDER) & (chip == GOAL)

                @pl.when(around)
                def _():
                    to_via(d).start()

                @pl.when(jnp.logical_not(around))
                def _():
                    to(d).start()

        return code // chips, requests_of(code // chips)

    def requests_of(code):
        chip = lax.rem(z + lax.rem(code, chips), chips)
        return tuple(
            request_of((chip * 2 + lax.rem(core + other, 2)) * slots + j)
            for other in range(2)
            for j in range(slots)
        )

    send_code = by_chip(SEND_ORDER, z, chips)
    twin = z * 2 + 1 - core
    loads[0].wait()
    first = requests_of(send_code)
    parts = (len(loads) - 4) // 2
    key_loads, value_loads = loads[1 : 1 + parts], loads[1 + parts : -3]
    for load in key_loads:
        load.wait()
    lax.fori_loop(0, chips - 1, serve, (send_code, first))
    fill(twin, [request_of(twin * slots + j) for j in range(slots)])
    to(twin).start()
    for load in loads[-3:]:
        load.wait()

    for j in range(slots):
        for s in range(STEPS):
            for h in range(own_heads):
                own_q[j, s * own_heads + h, :] = query_ref[
                    s, j, h * HD : (h + 1) * HD
                ].astype(jnp.float32)
    all_q[:, pl.ds(tp * rows, rows), :] = own_q[...].astype(jnp.bfloat16)
    for k in range(1, n_tp):
        q_copy(tp, lax.rem(tp + k, n_tp)).start()

    own = [request_of(me * slots + j) for j in range(slots)]
    for j in range(slots):
        for k in range(2):
            rec_ref[k, j, pl.ds(me * block, block), :] = raw[k][own[j]]

    def packed(tops, totals):
        bands = [both[j] for j in range(slots) for both in (tops, totals)]
        band = lax.broadcasted_iota(jnp.int32, bands[0].shape, 1) // (HD // len(bands))
        result = bands[0]
        for i in range(1, len(bands)):
            result = jnp.where(band == i, bands[i], result)
        return result

    new_tops, new_totals = [], []
    row_step = lax.broadcasted_iota(jnp.int32, (rows, HD), 0) // own_heads
    for j in range(slots):
        queries = own_q[j]
        scores = []
        for u in range(STEPS):
            key = new_ref[0, u, j, :].astype(jnp.float32).reshape(1, HD)
            dots = jnp.sum(queries * key, axis=1, keepdims=True)
            scores.append(jnp.where(row_step >= u, jnp.broadcast_to(dots, (rows, HD)), DEAD))
        top = scores[0]
        for u in range(1, STEPS):
            top = jnp.maximum(top, scores[u])
        total = jnp.zeros((rows, HD), jnp.float32)
        summed = jnp.zeros((rows, HD), jnp.float32)
        for u in range(STEPS):
            weight = jnp.exp((scores[u] - top) * SCALE)
            value = new_ref[1, u, j, :].astype(jnp.float32).reshape(1, HD)
            total = total + weight
            summed = summed + weight.astype(jnp.bfloat16).astype(jnp.float32) * value
        box[n_tp, j] = summed
        new_tops.append(top)
        new_totals.append(total)
    box[n_tp, slots] = packed(new_tops, new_totals)

    lengths = [len_ref[r] for r in own]
    mail[...] = jnp.zeros(mail.shape, jnp.float32)
    running[0] = jnp.full(running.shape[1:], FLOOR, jnp.float32)
    running[1] = jnp.zeros(running.shape[1:], jnp.float32)

    for k in range(1, n_tp):
        t = lax.rem(tp + k, n_tp)
        q_copy(t, t).wait_recv()

    span = 2 * block
    lane = lax.broadcasted_iota(jnp.int32, (n_tp * rows, span), 1)
    place = (lane // block) * (n_tp * block) + lax.rem(lane, block)

    def attend(chip):
        at = pl.ds(pl.multiple_of(chip * span, span), span)
        base = (chip * 2 * n_tp + tp) * block
        each = range(slots)
        scores = [
            lax.dot_general(
                all_q[j], rec_ref[0, j, at, :], (((1,), (1,)), ((), ())),
                preferred_element_type=jnp.float32,
            )
            for j in each
        ]
        scores = [jnp.where(place < lengths[j] - base, scores[j], DEAD) for j in each]
        before = [running[0, j] for j in each]
        top = [jnp.maximum(before[j], jnp.max(scores[j], axis=1, keepdims=True)) for j in each]
        weights = [
            jnp.exp((scores[j] - jnp.concatenate([top[j], top[j]], axis=1)) * SCALE) for j in each
        ]
        summed = [
            jnp.dot(
                weights[j].astype(jnp.bfloat16), rec_ref[1, j, at, :],
                preferred_element_type=jnp.float32,
            )
            for j in each
        ]
        shrink = [jnp.exp((before[j] - top[j]) * SCALE) for j in each]
        totals = [
            running[1, j] * shrink[j] + jnp.sum(weights[j], axis=1, keepdims=True) for j in each
        ]
        summed = [mail[j] * shrink[j] + summed[j] for j in each]
        for j in each:
            running[0, j] = top[j]
            running[1, j] = totals[j]
            mail[j] = summed[j]

    arrived(twin)
    attend(z)

    def collect(i, code):
        chip = lax.rem(z + lax.rem(code, chips), chips)
        arrived(chip * 2 + core)
        arrived(chip * 2 + 1 - core)
        attend(chip)
        return code // chips

    recv_code = by_chip(RECV_ORDER, z, chips)
    lax.fori_loop(0, chips - 1, collect, recv_code)

    mail[slots] = packed([running[0, j] for j in range(slots)], [running[1, j] for j in range(slots)])
    for k in sorted(range(1, n_tp), key=lambda k: -min(k, n_tp - k)):
        mail_copy(tp, lax.rem(tp + k, n_tp)).start()
    box[tp] = mail[:, pl.ds(tp * rows, rows), :]

    def sent(k, carry):
        to(lax.rem(me + k, n_ctx)).wait_send()
        return carry

    lax.fori_loop(1, n_ctx, sent, 0)

    @pl.when(z == VIA)
    def _():
        pass_on().wait_send()

    for k in range(1, n_tp):
        q_copy(tp, lax.rem(tp + k, n_tp)).wait_send()
    for k in range(1, n_tp):
        t = lax.rem(tp + k, n_tp)
        mail_copy(t, t).wait_recv()
        mail_copy(tp, t).wait_send()


def finish(rec_ref, box, out_ref, cache_ref, held, sem):
    copies = [
        pltpu.make_async_copy(rec_ref.at[k, j], cache_ref.at[k, j], sem.at[k, j])
        for k in range(rec_ref.shape[0])
        for j in range(rec_ref.shape[1])
    ]
    for copy in copies:
        copy.start()
    parts, rows = box.shape[0], box.shape[2]
    slots = box.shape[1] - 1
    band = HD // (2 * slots)
    own_heads = rows // STEPS
    results = []
    for j in range(slots):
        tops, totals = [], []
        for t in range(parts):
            bands = box[t, slots]
            at = 2 * j * band
            tops.append(jnp.broadcast_to(bands[:, at : at + 1], (rows, HD)))
            totals.append(jnp.broadcast_to(bands[:, at + band : at + band + 1], (rows, HD)))
        top = tops[0]
        for other in tops[1:]:
            top = jnp.maximum(top, other)
        total = jnp.zeros((rows, HD), jnp.float32)
        summed = jnp.zeros((rows, HD), jnp.float32)
        for t in range(parts):
            share = jnp.exp((tops[t] - top) * SCALE)
            total = total + totals[t] * share
            summed = summed + box[t, j] * share
        results.append(summed / total)
    for s in range(STEPS):
        for h in range(own_heads):
            r = s * own_heads + h
            piece = jnp.concatenate([result[r : r + 1] for result in results], axis=0)
            held[s, :, h * HD : (h + 1) * HD] = piece.astype(held.dtype)
    last = pltpu.make_async_copy(held, out_ref, sem.at[0, slots])
    last.start()
    last.wait()
    for copy in copies:
        copy.wait()


def shards(prefill_cache, lengths, slot_of, queries, new_kv):
    n_ctx, n_tp = lax.axis_size("ctx"), lax.axis_size("tp")
    _, requests, block, width = prefill_cache.shape
    slots = requests // n_ctx
    own_heads = queries.shape[2] // HD
    rows = STEPS * own_heads
    operands = (prefill_cache, slot_of, lengths, queries, new_kv)
    received, box = pl.pallas_call(
        kernel,
        out_shape=(
            jax.ShapeDtypeStruct((2, slots, n_ctx * block, width), jnp.bfloat16),
            jax.ShapeDtypeStruct((n_tp + 1, slots + 1, rows, HD), jnp.float32),
        ),
        in_specs=[pl.BlockSpec(memory_space=pltpu.HBM)] * len(operands),
        out_specs=(
            pl.BlockSpec(memory_space=pltpu.VMEM),
            pl.BlockSpec(memory_space=pltpu.VMEM),
        ),
        scratch_shapes=[
            pltpu.SMEM(slot_of.shape, jnp.int32),
            pltpu.SMEM(lengths.shape, jnp.int32),
            pltpu.VMEM(queries.shape, jnp.bfloat16),
            pltpu.VMEM(new_kv.shape, jnp.bfloat16),
            pltpu.VMEM(prefill_cache.shape[1:], jnp.bfloat16),
            pltpu.VMEM(prefill_cache.shape[1:], jnp.bfloat16),
            pltpu.VMEM((n_ctx, 2, slots, block, width), jnp.bfloat16),
            pltpu.VMEM((2, slots, block, width), jnp.bfloat16),
            pltpu.VMEM((slots, rows, HD), jnp.float32),
            pltpu.VMEM((slots, n_tp * rows, HD), jnp.bfloat16),
            pltpu.VMEM((slots + 1, n_tp * rows, HD), jnp.float32),
            pltpu.VMEM((2, slots, n_tp * rows, HD), jnp.float32),
            pltpu.SemaphoreType.DMA((4 + 2 * (requests // 8),)),
            pltpu.SemaphoreType.DMA((n_ctx,)),
            pltpu.SemaphoreType.DMA((n_ctx,)),
            pltpu.SemaphoreType.DMA((n_tp,)),
            pltpu.SemaphoreType.DMA((n_tp,)),
            pltpu.SemaphoreType.DMA((n_tp,)),
            pltpu.SemaphoreType.DMA((n_tp,)),
            pltpu.SemaphoreType.DMA((2,)),
            pltpu.SemaphoreType.REGULAR((n_ctx,)),
        ],
        compiler_params=pltpu.CompilerParams(
            collective_id=0, has_side_effects=True, vmem_limit_bytes=32 << 20
        ),
        name="handover",
    )(*(pltpu.with_memory_space_constraint(operand, pltpu.HBM) for operand in operands))
    return pl.pallas_call(
        finish,
        out_shape=(
            jax.ShapeDtypeStruct(queries.shape, jnp.bfloat16),
            jax.ShapeDtypeStruct(received.shape, jnp.bfloat16),
        ),
        in_specs=[pl.BlockSpec(memory_space=pltpu.VMEM)] * 2,
        out_specs=(pl.BlockSpec(memory_space=pltpu.HBM), pl.BlockSpec(memory_space=pltpu.HBM)),
        scratch_shapes=[
            pltpu.VMEM(queries.shape, jnp.bfloat16),
            pltpu.SemaphoreType.DMA((2, slots + 1)),
        ],
        compiler_params=pltpu.CompilerParams(vmem_limit_bytes=16 << 20),
        name="finish",
    )(received, box)


def solution(mesh):
    return jax.shard_map(
        shards,
        mesh=mesh,
        in_specs=(
            P(None, None, ("ctx", "tp"), "kvh"),
            P(),
            P(),
            P(None, "ctx", ("kvh", "tp")),
            P(None, None, "ctx", "kvh"),
        ),
        out_specs=(P(None, "ctx", ("kvh", "tp")), P(None, "ctx", "tp", "kvh")),
        check_vma=False,
    )
```

```python
import math

import jax
import jax.numpy as jnp
from jax import lax
from jax.experimental import pallas as pl
from jax.experimental.pallas import tpu as pltpu
from jax.sharding import PartitionSpec as P

HD = 128
STEPS = 4
SCALE = 1.0 / math.sqrt(HD)
MESH = pl.DeviceIdType.MESH
DEAD = -1e38
FLOOR = -1e30

SEND_ORDER = (
    (3, 5, 2, 7, 1, 4, 6),
    (2, 1, 4, 7, 6, 5, 3),
    (1, 3, 7, 6, 2, 4, 5),
    (5, 1, 2, 3, 6, 7, 4),
    (5, 4, 2, 6, 7, 1, 3),
    (3, 4, 7, 1, 5, 2, 6),
    (6, 2, 5, 3, 1, 4, 7),
    (1, 5, 4, 2, 6, 7, 3),
)
HOLDER, VIA, GOAL, TURN = 4, 3, 0, 4
RECV_ORDER = (
    (1, 5, 3, 6, 4, 7, 2),
    (4, 3, 7, 1, 5, 2, 6),
    (6, 2, 7, 1, 5, 3, 4),
    (5, 7, 6, 4, 3, 2, 1),
    (7, 1, 3, 4, 2, 5, 6),
    (4, 6, 3, 5, 7, 2, 1),
    (6, 7, 3, 2, 4, 1, 5),
    (2, 1, 6, 5, 7, 3, 4),
)


def by_chip(orders, z, radix):
    code = jnp.int32(0)
    for chip, order in enumerate(orders):
        number = sum(distance * radix**i for i, distance in enumerate(order))
        code = code + jnp.where(z == chip, number, 0)
    return code


def kernel(
    cache_in, slot_in, len_in, query_in, new_in,
    rec_ref, box,
    slot_ref, len_ref, query_ref, new_ref, raw_keys, raw_values, stage, passing, own_q, all_q, mail, running,
    load_sem, send_sem, recv_sem, q_send_sem, q_recv_sem, mail_send_sem, mail_recv_sem, pass_sem, ready,
):
    me = lax.axis_index("ctx")
    tp = lax.axis_index("tp")
    z, core = me // 2, lax.rem(me, 2)
    n_ctx = lax.axis_size("ctx")
    n_tp = lax.axis_size("tp")
    chips = n_ctx // 2
    requests = slot_ref.shape[0]
    slots = requests // n_ctx
    block = raw_keys.shape[1]
    raw = (raw_keys, raw_values)
    own_heads = query_ref.shape[2] // HD
    rows = STEPS * own_heads

    loads = [
        pltpu.make_async_copy(source, target, load_sem.at[i])
        for i, (source, target) in enumerate(
            [(slot_in, slot_ref)]
            + [(cache_in.at[k, pl.ds(i * 8, 8)], raw[k].at[pl.ds(i * 8, 8)]) for k in range(2) for i in range(requests // 8)]
            + [(query_in, query_ref), (len_in, len_ref), (new_in, new_ref)]
        )
    ]
    for load in loads:
        load.start()

    barrier = pltpu.get_barrier_semaphore()
    for k in range(1, n_tp):
        pl.semaphore_signal(
            barrier, inc=1, device_id={"tp": lax.rem(tp + k, n_tp)}, device_id_type=MESH
        )
    for d in range(n_ctx):

        @pl.when((d // 2 >= z) & (d != me))
        def _():
            pl.semaphore_signal(barrier, inc=1, device_id={"ctx": d}, device_id_type=MESH)

    pl.semaphore_wait(barrier, 2 * z + 1 + n_tp - 1)
    for d in range(n_ctx - 2):

        @pl.when(d // 2 < z)
        def _():
            pl.semaphore_signal(ready.at[me], inc=1, device_id={"ctx": d}, device_id_type=MESH)

    def request_of(slot):
        found = jnp.int32(0)
        for r in range(1, requests):
            found = jnp.where(slot_ref[r] == slot, r, found)
        return found

    def fill(d, found, kinds=range(2)):
        for j in range(slots):
            for k in kinds:
                stage[d, k, j] = raw[k][found[j]]

    def to(d):
        return pltpu.make_async_remote_copy(
            src_ref=stage.at[d],
            dst_ref=rec_ref.at[:, :, pl.ds(me * block, block)],
            send_sem=send_sem.at[d],
            recv_sem=recv_sem.at[me],
            device_id={"ctx": d},
            device_id_type=MESH,
        )

    def part_to(d, k):
        return pltpu.make_async_remote_copy(
            src_ref=stage.at[d, k],
            dst_ref=rec_ref.at[k, :, pl.ds(me * block, block)],
            send_sem=send_sem.at[d],
            recv_sem=recv_sem.at[me],
            device_id={"ctx": d},
            device_id_type=MESH,
        )

    round_parts = ((0, slots), (1, slots - 1))

    def to_via(d, k, count):
        return pltpu.make_async_remote_copy(
            src_ref=stage.at[d, k, pl.ds(0, count)],
            dst_ref=passing.at[k, pl.ds(0, count)],
            send_sem=send_sem.at[d],
            recv_sem=pass_sem.at[0, k],
            device_id={"ctx": VIA * 2 + core},
            device_id_type=MESH,
        )

    def pass_on(k, count):
        source = HOLDER * 2 + core
        return pltpu.make_async_remote_copy(
            src_ref=passing.at[k, pl.ds(0, count)],
            dst_ref=rec_ref.at[k, pl.ds(0, count), pl.ds(source * block, block)],
            send_sem=pass_sem.at[1, k],
            recv_sem=recv_sem.at[source],
            device_id={"ctx": GOAL * 2 + 1 - core},
            device_id_type=MESH,
        )

    def last_values_to(d):
        return pltpu.make_async_remote_copy(
            src_ref=stage.at[d, 1, pl.ds(slots - 1, 1)],
            dst_ref=rec_ref.at[1, pl.ds(slots - 1, 1), pl.ds(me * block, block)],
            send_sem=send_sem.at[d],
            recv_sem=recv_sem.at[me],
            device_id={"ctx": d},
            device_id_type=MESH,
        )

    def arrived(d):
        pltpu.make_async_remote_copy(
            src_ref=stage.at[d],
            dst_ref=rec_ref.at[:, :, pl.ds(d * block, block)],
            send_sem=send_sem.at[d],
            recv_sem=recv_sem.at[d],
            device_id={"ctx": d},
            device_id_type=MESH,
        ).wait_recv()

    def q_copy(owner, t):
        here = all_q.at[:, pl.ds(owner * rows, rows)]
        return pltpu.make_async_remote_copy(
            src_ref=here, dst_ref=here,
            send_sem=q_send_sem.at[t], recv_sem=q_recv_sem.at[owner],
            device_id={"tp": t}, device_id_type=MESH,
        )

    def mail_copy(owner, t):
        return pltpu.make_async_remote_copy(
            src_ref=mail.at[:, pl.ds(t * rows, rows)], dst_ref=box.at[owner],
            send_sem=mail_send_sem.at[t], recv_sem=mail_recv_sem.at[owner],
            device_id={"tp": t}, device_id_type=MESH,
        )

    def serve(i, carry):
        code, now = carry

        @pl.when((z == VIA) & (i == TURN))
        def _():
            for k, count in round_parts:
                to_via(GOAL * 2 + 1 - core, k, count).wait_recv()
                pass_on(k, count).start()

        chip = lax.rem(z + lax.rem(code, chips), chips)
        for other in range(2):
            d = chip * 2 + lax.rem(core + other, 2)

            @pl.when(chip > z)
            def _():
                pl.semaphore_wait(ready.at[d], 1)

            found = now[other * slots : (other + 1) * slots]
            if other == 0:
                fill(d, found, [0])
                part_to(d, 0).start()

                @pl.when(i == 0)
                def _():
                    for load in value_loads:
                        load.wait()

                fill(d, found, [1])
                part_to(d, 1).start()
            else:
                fill(d, found)
                around = (z == HOLDER) & (chip == GOAL)

                @pl.when(around)
                def _():
                    for k, count in round_parts:
                        to_via(d, k, count).start()
                    last_values_to(d).start()

                @pl.when(jnp.logical_not(around))
                def _():
                    to(d).start()

        return code // chips, requests_of(code // chips)

    def requests_of(code):
        chip = lax.rem(z + lax.rem(code, chips), chips)
        return tuple(
            request_of((chip * 2 + lax.rem(core + other, 2)) * slots + j)
            for other in range(2)
            for j in range(slots)
        )

    send_code = by_chip(SEND_ORDER, z, chips)
    twin = z * 2 + 1 - core
    loads[0].wait()
    first = requests_of(send_code)
    parts = (len(loads) - 4) // 2
    key_loads, value_loads = loads[1 : 1 + parts], loads[1 + parts : -3]
    for load in key_loads:
        load.wait()
    lax.fori_loop(0, chips - 1, serve, (send_code, first))
    fill(twin, [request_of(twin * slots + j) for j in range(slots)])
    to(twin).start()
    for load in loads[-3:]:
        load.wait()

    for j in range(slots):
        for s in range(STEPS):
            for h in range(own_heads):
                own_q[j, s * own_heads + h, :] = query_ref[
                    s, j, h * HD : (h + 1) * HD
                ].astype(jnp.float32)
    all_q[:, pl.ds(tp * rows, rows), :] = own_q[...].astype(jnp.bfloat16)
    for k in range(1, n_tp):
        q_copy(tp, lax.rem(tp + k, n_tp)).start()

    own = [request_of(me * slots + j) for j in range(slots)]
    for j in range(slots):
        for k in range(2):
            rec_ref[k, j, pl.ds(me * block, block), :] = raw[k][own[j]]

    def packed(tops, totals):
        bands = [both[j] for j in range(slots) for both in (tops, totals)]
        band = lax.broadcasted_iota(jnp.int32, bands[0].shape, 1) // (HD // len(bands))
        result = bands[0]
        for i in range(1, len(bands)):
            result = jnp.where(band == i, bands[i], result)
        return result

    new_tops, new_totals = [], []
    row_step = lax.broadcasted_iota(jnp.int32, (rows, HD), 0) // own_heads
    for j in range(slots):
        queries = own_q[j]
        scores = []
        for u in range(STEPS):
            key = new_ref[0, u, j, :].astype(jnp.float32).reshape(1, HD)
            dots = jnp.sum(queries * key, axis=1, keepdims=True)
            scores.append(jnp.where(row_step >= u, jnp.broadcast_to(dots, (rows, HD)), DEAD))
        top = scores[0]
        for u in range(1, STEPS):
            top = jnp.maximum(top, scores[u])
        total = jnp.zeros((rows, HD), jnp.float32)
        summed = jnp.zeros((rows, HD), jnp.float32)
        for u in range(STEPS):
            weight = jnp.exp((scores[u] - top) * SCALE)
            value = new_ref[1, u, j, :].astype(jnp.float32).reshape(1, HD)
            total = total + weight
            summed = summed + weight.astype(jnp.bfloat16).astype(jnp.float32) * value
        box[n_tp, j] = summed
        new_tops.append(top)
        new_totals.append(total)
    box[n_tp, slots] = packed(new_tops, new_totals)

    lengths = [len_ref[r] for r in own]
    mail[...] = jnp.zeros(mail.shape, jnp.float32)
    running[0] = jnp.full(running.shape[1:], FLOOR, jnp.float32)
    running[1] = jnp.zeros(running.shape[1:], jnp.float32)

    for k in range(1, n_tp):
        t = lax.rem(tp + k, n_tp)
        q_copy(t, t).wait_recv()

    span = 2 * block
    lane = lax.broadcasted_iota(jnp.int32, (n_tp * rows, span), 1)
    place = (lane // block) * (n_tp * block) + lax.rem(lane, block)

    def attend(chip):
        at = pl.ds(pl.multiple_of(chip * span, span), span)
        base = (chip * 2 * n_tp + tp) * block
        each = range(slots)
        scores = [
            lax.dot_general(
                all_q[j], rec_ref[0, j, at, :], (((1,), (1,)), ((), ())),
                preferred_element_type=jnp.float32,
            )
            for j in each
        ]
        scores = [jnp.where(place < lengths[j] - base, scores[j], DEAD) for j in each]
        before = [running[0, j] for j in each]
        top = [jnp.maximum(before[j], jnp.max(scores[j], axis=1, keepdims=True)) for j in each]
        weights = [
            jnp.exp((scores[j] - jnp.concatenate([top[j], top[j]], axis=1)) * SCALE) for j in each
        ]
        summed = [
            jnp.dot(
                weights[j].astype(jnp.bfloat16), rec_ref[1, j, at, :],
                preferred_element_type=jnp.float32,
            )
            for j in each
        ]
        shrink = [jnp.exp((before[j] - top[j]) * SCALE) for j in each]
        totals = [
            running[1, j] * shrink[j] + jnp.sum(weights[j], axis=1, keepdims=True) for j in each
        ]
        summed = [mail[j] * shrink[j] + summed[j] for j in each]
        for j in each:
            running[0, j] = top[j]
            running[1, j] = totals[j]
            mail[j] = summed[j]

    arrived(twin)
    attend(z)

    def collect(i, code):
        chip = lax.rem(z + lax.rem(code, chips), chips)
        arrived(chip * 2 + core)
        arrived(chip * 2 + 1 - core)
        attend(chip)
        return code // chips

    recv_code = by_chip(RECV_ORDER, z, chips)
    lax.fori_loop(0, chips - 1, collect, recv_code)

    mail[slots] = packed([running[0, j] for j in range(slots)], [running[1, j] for j in range(slots)])
    for k in sorted(range(1, n_tp), key=lambda k: -min(k, n_tp - k)):
        mail_copy(tp, lax.rem(tp + k, n_tp)).start()
    box[tp] = mail[:, pl.ds(tp * rows, rows), :]

    def sent(k, carry):
        to(lax.rem(me + k, n_ctx)).wait_send()
        return carry

    lax.fori_loop(1, n_ctx, sent, 0)

    @pl.when(z == VIA)
    def _():
        for k, count in round_parts:
            pass_on(k, count).wait_send()

    for k in range(1, n_tp):
        q_copy(tp, lax.rem(tp + k, n_tp)).wait_send()
    for k in range(1, n_tp):
        t = lax.rem(tp + k, n_tp)
        mail_copy(t, t).wait_recv()
        mail_copy(tp, t).wait_send()


def finish(rec_ref, box, out_ref, cache_ref, held, sem):
    copies = [
        pltpu.make_async_copy(rec_ref.at[k, j], cache_ref.at[k, j], sem.at[k, j])
        for k in range(rec_ref.shape[0])
        for j in range(rec_ref.shape[1])
    ]
    for copy in copies:
        copy.start()
    parts, rows = box.shape[0], box.shape[2]
    slots = box.shape[1] - 1
    band = HD // (2 * slots)
    own_heads = rows // STEPS
    results = []
    for j in range(slots):
        tops, totals = [], []
        for t in range(parts):
            bands = box[t, slots]
            at = 2 * j * band
            tops.append(jnp.broadcast_to(bands[:, at : at + 1], (rows, HD)))
            totals.append(jnp.broadcast_to(bands[:, at + band : at + band + 1], (rows, HD)))
        top = tops[0]
        for other in tops[1:]:
            top = jnp.maximum(top, other)
        total = jnp.zeros((rows, HD), jnp.float32)
        summed = jnp.zeros((rows, HD), jnp.float32)
        for t in range(parts):
            share = jnp.exp((tops[t] - top) * SCALE)
            total = total + totals[t] * share
            summed = summed + box[t, j] * share
        results.append(summed / total)
    for s in range(STEPS):
        for h in range(own_heads):
            r = s * own_heads + h
            piece = jnp.concatenate([result[r : r + 1] for result in results], axis=0)
            held[s, :, h * HD : (h + 1) * HD] = piece.astype(held.dtype)
    last = pltpu.make_async_copy(held, out_ref, sem.at[0, slots])
    last.start()
    last.wait()
    for copy in copies:
        copy.wait()


def shards(prefill_cache, lengths, slot_of, queries, new_kv):
    n_ctx, n_tp = lax.axis_size("ctx"), lax.axis_size("tp")
    _, requests, block, width = prefill_cache.shape
    slots = requests // n_ctx
    own_heads = queries.shape[2] // HD
    rows = STEPS * own_heads
    operands = (prefill_cache, slot_of, lengths, queries, new_kv)
    received, box = pl.pallas_call(
        kernel,
        out_shape=(
            jax.ShapeDtypeStruct((2, slots, n_ctx * block, width), jnp.bfloat16),
            jax.ShapeDtypeStruct((n_tp + 1, slots + 1, rows, HD), jnp.float32),
        ),
        in_specs=[pl.BlockSpec(memory_space=pltpu.HBM)] * len(operands),
        out_specs=(
            pl.BlockSpec(memory_space=pltpu.VMEM),
            pl.BlockSpec(memory_space=pltpu.VMEM),
        ),
        scratch_shapes=[
            pltpu.SMEM(slot_of.shape, jnp.int32),
            pltpu.SMEM(lengths.shape, jnp.int32),
            pltpu.VMEM(queries.shape, jnp.bfloat16),
            pltpu.VMEM(new_kv.shape, jnp.bfloat16),
            pltpu.VMEM(prefill_cache.shape[1:], jnp.bfloat16),
            pltpu.VMEM(prefill_cache.shape[1:], jnp.bfloat16),
            pltpu.VMEM((n_ctx, 2, slots, block, width), jnp.bfloat16),
            pltpu.VMEM((2, slots, block, width), jnp.bfloat16),
            pltpu.VMEM((slots, rows, HD), jnp.float32),
            pltpu.VMEM((slots, n_tp * rows, HD), jnp.bfloat16),
            pltpu.VMEM((slots + 1, n_tp * rows, HD), jnp.float32),
            pltpu.VMEM((2, slots, n_tp * rows, HD), jnp.float32),
            pltpu.SemaphoreType.DMA((4 + 2 * (requests // 8),)),
            pltpu.SemaphoreType.DMA((n_ctx,)),
            pltpu.SemaphoreType.DMA((n_ctx,)),
            pltpu.SemaphoreType.DMA((n_tp,)),
            pltpu.SemaphoreType.DMA((n_tp,)),
            pltpu.SemaphoreType.DMA((n_tp,)),
            pltpu.SemaphoreType.DMA((n_tp,)),
            pltpu.SemaphoreType.DMA((2, 2)),
            pltpu.SemaphoreType.REGULAR((n_ctx,)),
        ],
        compiler_params=pltpu.CompilerParams(
            collective_id=0, has_side_effects=True, vmem_limit_bytes=32 << 20
        ),
        name="handover",
    )(*(pltpu.with_memory_space_constraint(operand, pltpu.HBM) for operand in operands))
    return pl.pallas_call(
        finish,
        out_shape=(
            jax.ShapeDtypeStruct(queries.shape, jnp.bfloat16),
            jax.ShapeDtypeStruct(received.shape, jnp.bfloat16),
        ),
        in_specs=[pl.BlockSpec(memory_space=pltpu.VMEM)] * 2,
        out_specs=(pl.BlockSpec(memory_space=pltpu.HBM), pl.BlockSpec(memory_space=pltpu.HBM)),
        scratch_shapes=[
            pltpu.VMEM(queries.shape, jnp.bfloat16),
            pltpu.SemaphoreType.DMA((2, slots + 1)),
        ],
        compiler_params=pltpu.CompilerParams(vmem_limit_bytes=16 << 20),
        name="finish",
    )(received, box)


def solution(mesh):
    return jax.shard_map(
        shards,
        mesh=mesh,
        in_specs=(
            P(None, None, ("ctx", "tp"), "kvh"),
            P(),
            P(),
            P(None, "ctx", ("kvh", "tp")),
            P(None, None, "ctx", "kvh"),
        ),
        out_specs=(P(None, "ctx", ("kvh", "tp")), P(None, "ctx", "tp", "kvh")),
        check_vma=False,
    )
```

```python
import math

import jax
import jax.numpy as jnp
from jax import lax
from jax.experimental import pallas as pl
from jax.experimental.pallas import tpu as pltpu
from jax.sharding import PartitionSpec as P

HD = 128
STEPS = 4
SCALE = 1.0 / math.sqrt(HD)
MESH = pl.DeviceIdType.MESH
DEAD = -1e38
FLOOR = -1e30

SEND_ORDER = (
    (3, 5, 2, 4, 6, 1, 7),
    (7, 3, 6, 5, 4, 1, 2),
    (1, 7, 4, 2, 6, 3, 5),
    (6, 1, 2, 5, 7, 4, 3),
    (6, 4, 2, 5, 3, 7, 1),
    (3, 4, 5, 7, 1, 6, 2),
    (6, 5, 3, 1, 7, 2, 4),
    (2, 6, 1, 5, 4, 3, 7),
)
HOLDER, VIA, GOAL, TURN = 4, 3, 0, 4
RECV_ORDER = (
    (1, 2, 7, 5, 3, 6, 4),
    (4, 1, 5, 2, 6, 7, 3),
    (2, 6, 3, 7, 1, 5, 4),
    (5, 7, 3, 6, 4, 2, 1),
    (7, 2, 5, 4, 1, 3, 6),
    (2, 3, 7, 6, 4, 5, 1),
    (6, 3, 4, 2, 7, 1, 5),
    (2, 7, 5, 1, 3, 6, 4),
)


def by_chip(orders, z, radix):
    code = jnp.int32(0)
    for chip, order in enumerate(orders):
        number = sum(distance * radix**i for i, distance in enumerate(order))
        code = code + jnp.where(z == chip, number, 0)
    return code


def kernel(
    cache_in, slot_in, len_in, query_in, new_in,
    rec_ref, box,
    slot_ref, len_ref, query_ref, new_ref, raw_keys, raw_values, stage, passing, own_q, all_q, mail, running,
    load_sem, send_sem, recv_sem, q_send_sem, q_recv_sem, mail_send_sem, mail_recv_sem, pass_sem, ready,
):
    me = lax.axis_index("ctx")
    tp = lax.axis_index("tp")
    z, core = me // 2, lax.rem(me, 2)
    n_ctx = lax.axis_size("ctx")
    n_tp = lax.axis_size("tp")
    chips = n_ctx // 2
    requests = slot_ref.shape[0]
    slots = requests // n_ctx
    block = raw_keys.shape[1]
    raw = (raw_keys, raw_values)
    own_heads = query_ref.shape[2] // HD
    rows = STEPS * own_heads

    loads = [
        pltpu.make_async_copy(source, target, load_sem.at[i])
        for i, (source, target) in enumerate(
            [(slot_in, slot_ref)]
            + [(cache_in.at[k, pl.ds(i * 8, 8)], raw[k].at[pl.ds(i * 8, 8)]) for k in range(2) for i in range(requests // 8)]
            + [(query_in, query_ref), (len_in, len_ref), (new_in, new_ref)]
        )
    ]
    for load in loads:
        load.start()

    barrier = pltpu.get_barrier_semaphore()
    for k in range(1, n_tp):
        pl.semaphore_signal(
            barrier, inc=1, device_id={"tp": lax.rem(tp + k, n_tp)}, device_id_type=MESH
        )
    for d in range(n_ctx):

        @pl.when((d // 2 >= z) & (d != me))
        def _():
            pl.semaphore_signal(barrier, inc=1, device_id={"ctx": d}, device_id_type=MESH)

    pl.semaphore_wait(barrier, 2 * z + 1 + n_tp - 1)
    for d in range(n_ctx - 2):

        @pl.when(d // 2 < z)
        def _():
            pl.semaphore_signal(ready.at[me], inc=1, device_id={"ctx": d}, device_id_type=MESH)

    def request_of(slot):
        found = jnp.int32(0)
        for r in range(1, requests):
            found = jnp.where(slot_ref[r] == slot, r, found)
        return found

    def fill(d, found, kinds=range(2)):
        for j in range(slots):
            for k in kinds:
                stage[d, k, j] = raw[k][found[j]]

    def to(d):
        return pltpu.make_async_remote_copy(
            src_ref=stage.at[d],
            dst_ref=rec_ref.at[:, :, pl.ds(me * block, block)],
            send_sem=send_sem.at[d],
            recv_sem=recv_sem.at[me],
            device_id={"ctx": d},
            device_id_type=MESH,
        )

    def part_to(d, k):
        return pltpu.make_async_remote_copy(
            src_ref=stage.at[d, k],
            dst_ref=rec_ref.at[k, :, pl.ds(me * block, block)],
            send_sem=send_sem.at[d],
            recv_sem=recv_sem.at[me],
            device_id={"ctx": d},
            device_id_type=MESH,
        )

    round_parts = ((0, slots), (1, slots - 1))

    def to_via(d, k, count):
        return pltpu.make_async_remote_copy(
            src_ref=stage.at[d, k, pl.ds(0, count)],
            dst_ref=passing.at[k, pl.ds(0, count)],
            send_sem=send_sem.at[d],
            recv_sem=pass_sem.at[0, k],
            device_id={"ctx": VIA * 2 + core},
            device_id_type=MESH,
        )

    def pass_on(k, count):
        source = HOLDER * 2 + core
        return pltpu.make_async_remote_copy(
            src_ref=passing.at[k, pl.ds(0, count)],
            dst_ref=rec_ref.at[k, pl.ds(0, count), pl.ds(source * block, block)],
            send_sem=pass_sem.at[1, k],
            recv_sem=recv_sem.at[source],
            device_id={"ctx": GOAL * 2 + 1 - core},
            device_id_type=MESH,
        )

    def last_values_to(d):
        return pltpu.make_async_remote_copy(
            src_ref=stage.at[d, 1, pl.ds(slots - 1, 1)],
            dst_ref=rec_ref.at[1, pl.ds(slots - 1, 1), pl.ds(me * block, block)],
            send_sem=send_sem.at[d],
            recv_sem=recv_sem.at[me],
            device_id={"ctx": d},
            device_id_type=MESH,
        )

    def arrived(d):
        pltpu.make_async_remote_copy(
            src_ref=stage.at[d],
            dst_ref=rec_ref.at[:, :, pl.ds(d * block, block)],
            send_sem=send_sem.at[d],
            recv_sem=recv_sem.at[d],
            device_id={"ctx": d},
            device_id_type=MESH,
        ).wait_recv()

    def q_copy(owner, t):
        here = all_q.at[:, pl.ds(owner * rows, rows)]
        return pltpu.make_async_remote_copy(
            src_ref=here, dst_ref=here,
            send_sem=q_send_sem.at[t], recv_sem=q_recv_sem.at[owner],
            device_id={"tp": t}, device_id_type=MESH,
        )

    def mail_copy(owner, t):
        return pltpu.make_async_remote_copy(
            src_ref=mail.at[:, pl.ds(t * rows, rows)], dst_ref=box.at[owner],
            send_sem=mail_send_sem.at[t], recv_sem=mail_recv_sem.at[owner],
            device_id={"tp": t}, device_id_type=MESH,
        )

    def serve(i, carry):
        code, now = carry

        @pl.when((z == VIA) & (i == TURN))
        def _():
            for k, count in round_parts:
                to_via(GOAL * 2 + 1 - core, k, count).wait_recv()
                pass_on(k, count).start()

        chip = lax.rem(z + lax.rem(code, chips), chips)
        for other in range(2):
            d = chip * 2 + lax.rem(core + other, 2)

            @pl.when(chip > z)
            def _():
                pl.semaphore_wait(ready.at[d], 1)

            found = now[other * slots : (other + 1) * slots]
            if other == 0:
                fill(d, found, [0])
                part_to(d, 0).start()

                @pl.when(i == 0)
                def _():
                    for load in value_loads:
                        load.wait()

                fill(d, found, [1])
                part_to(d, 1).start()
            else:
                fill(d, found)
                around = (z == HOLDER) & (chip == GOAL)

                @pl.when(around)
                def _():
                    for k, count in round_parts:
                        to_via(d, k, count).start()
                    last_values_to(d).start()

                @pl.when(jnp.logical_not(around))
                def _():
                    to(d).start()

        return code // chips, requests_of(code // chips)

    def requests_of(code):
        chip = lax.rem(z + lax.rem(code, chips), chips)
        return tuple(
            request_of((chip * 2 + lax.rem(core + other, 2)) * slots + j)
            for other in range(2)
            for j in range(slots)
        )

    send_code = by_chip(SEND_ORDER, z, chips)
    twin = z * 2 + 1 - core
    loads[0].wait()
    first = requests_of(send_code)
    parts = (len(loads) - 4) // 2
    key_loads, value_loads = loads[1 : 1 + parts], loads[1 + parts : -3]
    for load in key_loads:
        load.wait()
    lax.fori_loop(0, chips - 1, serve, (send_code, first))
    fill(twin, [request_of(twin * slots + j) for j in range(slots)])
    to(twin).start()
    for load in loads[-3:]:
        load.wait()

    for j in range(slots):
        for s in range(STEPS):
            for h in range(own_heads):
                own_q[j, s * own_heads + h, :] = query_ref[
                    s, j, h * HD : (h + 1) * HD
                ].astype(jnp.float32)
    all_q[:, pl.ds(tp * rows, rows), :] = own_q[...].astype(jnp.bfloat16)
    for k in range(1, n_tp):
        q_copy(tp, lax.rem(tp + k, n_tp)).start()

    own = [request_of(me * slots + j) for j in range(slots)]
    for j in range(slots):
        for k in range(2):
            rec_ref[k, j, pl.ds(me * block, block), :] = raw[k][own[j]]

    def packed(tops, totals):
        bands = [both[j] for j in range(slots) for both in (tops, totals)]
        band = lax.broadcasted_iota(jnp.int32, bands[0].shape, 1) // (HD // len(bands))
        result = bands[0]
        for i in range(1, len(bands)):
            result = jnp.where(band == i, bands[i], result)
        return result

    new_tops, new_totals = [], []
    row_step = lax.broadcasted_iota(jnp.int32, (rows, HD), 0) // own_heads
    for j in range(slots):
        queries = own_q[j]
        scores = []
        for u in range(STEPS):
            key = new_ref[0, u, j, :].astype(jnp.float32).reshape(1, HD)
            dots = jnp.sum(queries * key, axis=1, keepdims=True)
            scores.append(jnp.where(row_step >= u, jnp.broadcast_to(dots, (rows, HD)), DEAD))
        top = scores[0]
        for u in range(1, STEPS):
            top = jnp.maximum(top, scores[u])
        total = jnp.zeros((rows, HD), jnp.float32)
        summed = jnp.zeros((rows, HD), jnp.float32)
        for u in range(STEPS):
            weight = jnp.exp((scores[u] - top) * SCALE)
            value = new_ref[1, u, j, :].astype(jnp.float32).reshape(1, HD)
            total = total + weight
            summed = summed + weight.astype(jnp.bfloat16).astype(jnp.float32) * value
        box[n_tp, j] = summed
        new_tops.append(top)
        new_totals.append(total)
    box[n_tp, slots] = packed(new_tops, new_totals)

    lengths = [len_ref[r] for r in own]
    mail[...] = jnp.zeros(mail.shape, jnp.float32)
    running[0] = jnp.full(running.shape[1:], FLOOR, jnp.float32)
    running[1] = jnp.zeros(running.shape[1:], jnp.float32)

    for k in range(1, n_tp):
        t = lax.rem(tp + k, n_tp)
        q_copy(t, t).wait_recv()

    span = 2 * block
    lane = lax.broadcasted_iota(jnp.int32, (n_tp * rows, span), 1)
    place = (lane // block) * (n_tp * block) + lax.rem(lane, block)

    def attend(chip):
        at = pl.ds(pl.multiple_of(chip * span, span), span)
        base = (chip * 2 * n_tp + tp) * block
        each = range(slots)
        scores = [
            lax.dot_general(
                all_q[j], rec_ref[0, j, at, :], (((1,), (1,)), ((), ())),
                preferred_element_type=jnp.float32,
            )
            for j in each
        ]
        scores = [jnp.where(place < lengths[j] - base, scores[j], DEAD) for j in each]
        before = [running[0, j] for j in each]
        top = [jnp.maximum(before[j], jnp.max(scores[j], axis=1, keepdims=True)) for j in each]
        weights = [
            jnp.exp((scores[j] - jnp.concatenate([top[j], top[j]], axis=1)) * SCALE) for j in each
        ]
        summed = [
            jnp.dot(
                weights[j].astype(jnp.bfloat16), rec_ref[1, j, at, :],
                preferred_element_type=jnp.float32,
            )
            for j in each
        ]
        shrink = [jnp.exp((before[j] - top[j]) * SCALE) for j in each]
        totals = [
            running[1, j] * shrink[j] + jnp.sum(weights[j], axis=1, keepdims=True) for j in each
        ]
        summed = [mail[j] * shrink[j] + summed[j] for j in each]
        for j in each:
            running[0, j] = top[j]
            running[1, j] = totals[j]
            mail[j] = summed[j]

    arrived(twin)
    attend(z)

    def collect(i, code):
        chip = lax.rem(z + lax.rem(code, chips), chips)
        arrived(chip * 2 + core)
        arrived(chip * 2 + 1 - core)
        attend(chip)
        return code // chips

    recv_code = by_chip(RECV_ORDER, z, chips)
    lax.fori_loop(0, chips - 1, collect, recv_code)

    mail[slots] = packed([running[0, j] for j in range(slots)], [running[1, j] for j in range(slots)])
    for k in sorted(range(1, n_tp), key=lambda k: -min(k, n_tp - k)):
        mail_copy(tp, lax.rem(tp + k, n_tp)).start()
    box[tp] = mail[:, pl.ds(tp * rows, rows), :]

    def sent(k, carry):
        to(lax.rem(me + k, n_ctx)).wait_send()
        return carry

    lax.fori_loop(1, n_ctx, sent, 0)

    @pl.when(z == VIA)
    def _():
        for k, count in round_parts:
            pass_on(k, count).wait_send()

    for k in range(1, n_tp):
        q_copy(tp, lax.rem(tp + k, n_tp)).wait_send()
    for k in range(1, n_tp):
        t = lax.rem(tp + k, n_tp)
        mail_copy(t, t).wait_recv()
        mail_copy(tp, t).wait_send()


def finish(rec_ref, box, out_ref, cache_ref, held, sem):
    copies = [
        pltpu.make_async_copy(rec_ref.at[k, j], cache_ref.at[k, j], sem.at[k, j])
        for k in range(rec_ref.shape[0])
        for j in range(rec_ref.shape[1])
    ]
    for copy in copies:
        copy.start()
    parts, rows = box.shape[0], box.shape[2]
    slots = box.shape[1] - 1
    band = HD // (2 * slots)
    own_heads = rows // STEPS
    results = []
    for j in range(slots):
        tops, totals = [], []
        for t in range(parts):
            bands = box[t, slots]
            at = 2 * j * band
            tops.append(jnp.broadcast_to(bands[:, at : at + 1], (rows, HD)))
            totals.append(jnp.broadcast_to(bands[:, at + band : at + band + 1], (rows, HD)))
        top = tops[0]
        for other in tops[1:]:
            top = jnp.maximum(top, other)
        total = jnp.zeros((rows, HD), jnp.float32)
        summed = jnp.zeros((rows, HD), jnp.float32)
        for t in range(parts):
            share = jnp.exp((tops[t] - top) * SCALE)
            total = total + totals[t] * share
            summed = summed + box[t, j] * share
        results.append(summed / total)
    for s in range(STEPS):
        for h in range(own_heads):
            r = s * own_heads + h
            piece = jnp.concatenate([result[r : r + 1] for result in results], axis=0)
            held[s, :, h * HD : (h + 1) * HD] = piece.astype(held.dtype)
    last = pltpu.make_async_copy(held, out_ref, sem.at[0, slots])
    last.start()
    last.wait()
    for copy in copies:
        copy.wait()


def shards(prefill_cache, lengths, slot_of, queries, new_kv):
    n_ctx, n_tp = lax.axis_size("ctx"), lax.axis_size("tp")
    _, requests, block, width = prefill_cache.shape
    slots = requests // n_ctx
    own_heads = queries.shape[2] // HD
    rows = STEPS * own_heads
    operands = (prefill_cache, slot_of, lengths, queries, new_kv)
    received, box = pl.pallas_call(
        kernel,
        out_shape=(
            jax.ShapeDtypeStruct((2, slots, n_ctx * block, width), jnp.bfloat16),
            jax.ShapeDtypeStruct((n_tp + 1, slots + 1, rows, HD), jnp.float32),
        ),
        in_specs=[pl.BlockSpec(memory_space=pltpu.HBM)] * len(operands),
        out_specs=(
            pl.BlockSpec(memory_space=pltpu.VMEM),
            pl.BlockSpec(memory_space=pltpu.VMEM),
        ),
        scratch_shapes=[
            pltpu.SMEM(slot_of.shape, jnp.int32),
            pltpu.SMEM(lengths.shape, jnp.int32),
            pltpu.VMEM(queries.shape, jnp.bfloat16),
            pltpu.VMEM(new_kv.shape, jnp.bfloat16),
            pltpu.VMEM(prefill_cache.shape[1:], jnp.bfloat16),
            pltpu.VMEM(prefill_cache.shape[1:], jnp.bfloat16),
            pltpu.VMEM((n_ctx, 2, slots, block, width), jnp.bfloat16),
            pltpu.VMEM((2, slots, block, width), jnp.bfloat16),
            pltpu.VMEM((slots, rows, HD), jnp.float32),
            pltpu.VMEM((slots, n_tp * rows, HD), jnp.bfloat16),
            pltpu.VMEM((slots + 1, n_tp * rows, HD), jnp.float32),
            pltpu.VMEM((2, slots, n_tp * rows, HD), jnp.float32),
            pltpu.SemaphoreType.DMA((4 + 2 * (requests // 8),)),
            pltpu.SemaphoreType.DMA((n_ctx,)),
            pltpu.SemaphoreType.DMA((n_ctx,)),
            pltpu.SemaphoreType.DMA((n_tp,)),
            pltpu.SemaphoreType.DMA((n_tp,)),
            pltpu.SemaphoreType.DMA((n_tp,)),
            pltpu.SemaphoreType.DMA((n_tp,)),
            pltpu.SemaphoreType.DMA((2, 2)),
            pltpu.SemaphoreType.REGULAR((n_ctx,)),
        ],
        compiler_params=pltpu.CompilerParams(
            collective_id=0, has_side_effects=True, vmem_limit_bytes=32 << 20
        ),
        name="handover",
    )(*(pltpu.with_memory_space_constraint(operand, pltpu.HBM) for operand in operands))
    return pl.pallas_call(
        finish,
        out_shape=(
            jax.ShapeDtypeStruct(queries.shape, jnp.bfloat16),
            jax.ShapeDtypeStruct(received.shape, jnp.bfloat16),
        ),
        in_specs=[pl.BlockSpec(memory_space=pltpu.VMEM)] * 2,
        out_specs=(pl.BlockSpec(memory_space=pltpu.HBM), pl.BlockSpec(memory_space=pltpu.HBM)),
        scratch_shapes=[
            pltpu.VMEM(queries.shape, jnp.bfloat16),
            pltpu.SemaphoreType.DMA((2, slots + 1)),
        ],
        compiler_params=pltpu.CompilerParams(vmem_limit_bytes=16 << 20),
        name="finish",
    )(received, box)


def solution(mesh):
    return jax.shard_map(
        shards,
        mesh=mesh,
        in_specs=(
            P(None, None, ("ctx", "tp"), "kvh"),
            P(),
            P(),
            P(None, "ctx", ("kvh", "tp")),
            P(None, None, "ctx", "kvh"),
        ),
        out_specs=(P(None, "ctx", ("kvh", "tp")), P(None, "ctx", "tp", "kvh")),
        check_vma=False,
    )
```
